256 devices in a mesh: gx: 4 (over x), gy: 4 (over y), gz: 16 (over z, core).
Axes of the slice: x: 4, y: 4, z: 8, core: 2. Of those that a mesh axis runs over, the one named last changes fastest.
Arguments:
- positions: float32 [3, 8, 8, 2048], P(None, 'gx', 'gy', 'gz'), may hold values from -0.5 to 0.5
- velocities: float32 [3, 8, 8, 2048], P(None, 'gx', 'gy', 'gz'), may hold values from -2 to 2
- forces_in: float32 [3, 8, 8, 2048], P(None, 'gx', 'gy', 'gz'), may hold values from -6 to 6
- counts: int32 [8, 8, 64], P('gx', 'gy', 'gz'), may hold values from 0 to 32, as said below
- neighbours: int32 [24, 8, 8, 2048], P(None, 'gx', 'gy', 'gz'), may hold values from 0 to 863, as said below
- send_list: int32 [4, 4, 8192], P('gx', 'gy', 'gz'), may hold values from -1 to 511, as said below
- w_radial: float32 [8, 128], replicated, may hold values from -2 to 2
- w_env: bfloat16 [128, 128], replicated, may hold values from -0.5 to 0.5
- w_latent: bfloat16 [256, 128], replicated, may hold values from -0.375 to 0.375
- w_out: bfloat16 [128], replicated, may hold values from -0.5 to 0.5
Outputs:
- positions_out: float32 [3, 8, 8, 2048], P(None, 'gx', 'gy', 'gz')
- velocities_out: float32 [3, 8, 8, 2048], P(None, 'gx', 'gy', 'gz')
- forces_out: float32 [3, 8, 8, 2048], P(None, 'gx', 'gy', 'gz')
- work_energy: float32 [4, 4, 8192], P('gx', 'gy', 'gz')
The draws below stay inside these ranges and needn't reach their ends.
Inputs may be any that keep to these rules, and one draw needn't show every extreme that they name: `counts`: A cell's occupied slots are its first ones. The devices of one gz group hold 4096 occupied slots together, and one of them has every slot occupied. `neighbours`: an entry never names the atom itself; entries naming unoccupied slots are padding. `send_list`: every occupied slot appears exactly once in its device's list, unoccupied ones never; each device receives exactly 256 atoms over all senders, and some sender fills all 32 rows for every receiver.
All inputs are finite; a program needn't handle non-finite values.
Results may differ from the reference program's by a relative error of at most 0.035.
Values sent between devices are 32-bit elements; how exact they have to be, the bound alone decides.
No kernel may reach another device: no remote copies, remote signals or barrier semaphores. Data moves between devices by JAX's collectives and lax.ppermute only.
A program may use at most 128 MiB of HBM per device.

```python
import jax
import jax.numpy as jnp
from jax import lax

CX = 2
CY = 2
CZ = 4
P_SIZE = 32
NBR = 24
FEAT = 128
BASIS = 8
STEPS = 2
NX = 8
NY = 8
NZ = 64
SLOTS = 512
WORK = 256
CAP = 32
N_GX = 4
N_GY = 4
N_GZ = 16


def build_layout(key):
    groups_x = NX // CX
    groups_y = NY // CY
    groups_z = NZ // CZ
    cell_total = CX * CY * CZ
    slot_total = cell_total * P_SIZE
    half_total = slot_total // 2
    key_list = jax.random.split(key, 4)
    full_rank = jax.random.randint(key_list[0], (groups_x, groups_y, 1), 0, groups_z)
    rank_list = jnp.arange(groups_z, dtype=jnp.int32).reshape(1, 1, groups_z)
    is_full = rank_list == full_rank
    shares_weight = jnp.where(is_full, 0, jax.random.randint(key_list[1], (groups_x, groups_y, groups_z), 500, 1001))
    remainder = groups_z * half_total - slot_total
    share = remainder * shares_weight // jnp.sum(shares_weight, axis=2, keepdims=True)
    leftover = remainder - jnp.sum(share, axis=2, keepdims=True)
    light_rank = jnp.cumsum(1 - is_full.astype(jnp.int32), axis=2) - 1
    extra = jnp.where(jnp.logical_and(jnp.logical_not(is_full), light_rank < leftover), 1, 0)
    occupied_total = jnp.where(is_full, slot_total, share + extra)
    scores = jax.random.randint(key_list[2], (groups_x, groups_y, groups_z, cell_total), 0, cell_total) * cell_total
    scores = scores + jnp.arange(cell_total, dtype=jnp.int32)
    cell_rank = jnp.argsort(jnp.argsort(scores, axis=3), axis=3)
    cell_count = jnp.clip(occupied_total[..., None] - P_SIZE * cell_rank, 0, P_SIZE)
    counts = cell_count.reshape(groups_x, groups_y, groups_z, CX, CY, CZ).transpose(0, 3, 1, 4, 2, 5).reshape(NX, NY, NZ)
    slot_live = jnp.arange(P_SIZE, dtype=jnp.int32).reshape(1, 1, 1, 1, P_SIZE) < cell_count[..., None]
    slot_live = slot_live.reshape(groups_x, groups_y, groups_z, slot_total)
    slot_iota = jnp.arange(slot_total, dtype=jnp.int32)
    picks = jax.random.randint(key_list[3], (groups_x, groups_y, groups_z, slot_total), 0, slot_total) * slot_total + slot_iota
    picks = jnp.where(slot_live, picks, slot_total * slot_total + slot_iota)
    position = jnp.argsort(jnp.argsort(picks, axis=3), axis=3)
    before = (jnp.cumsum(occupied_total, axis=2) - occupied_total)[..., None]
    global_rank = before + position
    receiver = global_rank % groups_z
    first_rank = before + (receiver - before) % groups_z
    place = (global_rank - first_rank) // groups_z
    capacity = slot_total // groups_z
    device_base = jnp.arange(groups_x * groups_y * groups_z, dtype=jnp.int32).reshape(groups_x, groups_y, groups_z, 1) * slot_total
    where_to = jnp.where(slot_live, device_base + receiver * capacity + place, groups_x * groups_y * groups_z * slot_total)
    values = jnp.broadcast_to(slot_iota, (groups_x, groups_y, groups_z, slot_total))
    sends = jnp.full((groups_x * groups_y * groups_z * slot_total,), -1, dtype=jnp.int32)
    sends = sends.at[where_to.reshape(-1)].set(values.reshape(-1), mode='drop')
    return (counts.astype(jnp.int32), sends.reshape(groups_x, groups_y, groups_z * slot_total))


def draw_counts(key, part):
    counts, sends = build_layout(key)
    return counts


def draw_send_list(key, part):
    counts, sends = build_layout(key)
    return sends


def draw_neighbours(key, part):
    counts, sends = build_layout(key)
    key = jax.random.fold_in(key, 7)
    key_list = jax.random.split(key, 3)
    shape = (NBR, NX, NY, NZ, P_SIZE)
    offset_code = jax.random.randint(key_list[0], shape, 0, 27)
    shift_x = offset_code // 9 - 1
    shift_y = offset_code // 3 % 3 - 1
    shift_z = offset_code % 3 - 1
    grid_x = jnp.arange(NX, dtype=jnp.int32).reshape(1, NX, 1, 1, 1)
    grid_y = jnp.arange(NY, dtype=jnp.int32).reshape(1, 1, NY, 1, 1)
    grid_z = jnp.arange(NZ, dtype=jnp.int32).reshape(1, 1, 1, NZ, 1)
    beside = counts[(grid_x + shift_x) % NX, (grid_y + shift_y) % NY, (grid_z + shift_z) % NZ]
    raw_value = jax.random.randint(key_list[1], shape, 0, 1048576)
    roaming = jax.random.randint(key_list[2], shape, 0, 4) == 0
    slot_pick = jnp.where(roaming, raw_value % P_SIZE, raw_value % jnp.maximum(beside, 1))
    own_slot = jnp.arange(P_SIZE, dtype=jnp.int32).reshape(1, 1, 1, 1, P_SIZE)
    is_itself = jnp.logical_and(offset_code == 13, slot_pick == own_slot)
    slot_pick = jnp.where(is_itself, (slot_pick + 1) % P_SIZE, slot_pick)
    return (offset_code * P_SIZE + slot_pick).reshape(NBR, NX, NY, NZ * P_SIZE).astype(jnp.int32)


def block_levels(rng, shape, shards, least, high):
    def one(dim, parts):
        heights = jax.random.uniform(jax.random.fold_in(jax.random.fold_in(rng, 6), dim), (parts,), jnp.float32, least / len(shards), high / len(shards))
        return jnp.repeat(jnp.exp(heights), shape[dim] // parts).reshape((-1,) + (1,) * (len(shape) - dim - 1))

    factor_of = one(*shards[0])
    for cut in shards[1:]:
        factor_of = factor_of * one(*cut)
    return factor_of


def gaussian(own_key, shape, scale, limit, shards=(), kind=jnp.bfloat16):
    result = jax.random.normal(own_key, shape, jnp.float32) * scale
    if len(shards) > 0:
        result = block_levels(own_key, shape, shards, -0.22, 0.18) * result
    return jnp.clip(result, min=-limit, max=limit).astype(kind)


def setup_inputs(seed: int = 0) -> dict:
    splits = jax.random.split(jax.random.key(seed), 11)
    positions = jnp.clip(jax.random.uniform(splits[0], (3, NX, NY, NZ * P_SIZE), jnp.float32, -0.5, 0.5) * block_levels(splits[0], (3, NX, NY, NZ * P_SIZE), ((1, 4), (2, 4), (3, 16)), -0.4, 0.0), -0.5, 0.5)
    velocities = gaussian(splits[1], (3, NX, NY, NZ * P_SIZE), 0.3, 2.0, ((1, 4), (2, 4), (3, 16)), jnp.float32)
    forces_in = gaussian(splits[2], (3, NX, NY, NZ * P_SIZE), 1.0, 6.0, ((1, 4), (2, 4), (3, 16)), jnp.float32)
    counts = draw_counts(jax.random.fold_in(splits[10], 71), 0)
    neighbours = draw_neighbours(jax.random.fold_in(splits[10], 71), 0)
    send_list = draw_send_list(jax.random.fold_in(splits[10], 71), 0)
    w_radial = gaussian(splits[6], (BASIS, FEAT), BASIS ** -0.5, 2.0, (), jnp.float32)
    w_env = gaussian(splits[7], (FEAT, FEAT), FEAT ** -0.5, 0.5)
    w_latent = gaussian(splits[8], (2 * FEAT, FEAT), (2 * FEAT) ** -0.5, 0.375)
    w_out = gaussian(splits[9], (FEAT,), FEAT ** -0.5, 0.5)
    return dict(positions=positions, velocities=velocities, forces_in=forces_in, counts=counts, neighbours=neighbours, send_list=send_list, w_radial=w_radial, w_env=w_env, w_latent=w_latent, w_out=w_out)


CUTOFF_SQUARE = 4.0
CUTOFF_RADIUS = 2.0
SOFTENING = 0.25
BASIS_SHARPNESS = 4.0
CELL_LENGTH = 1.0
FAR_OFFSET = 3.0
TIME_STEP = 0.5

def site_energy(displace, w_radial, w_env, w_latent, w_out):
    neighbour_count = displace.shape[1]
    row_count = displace.shape[2]
    width = w_env.shape[0]
    basis_count = w_radial.shape[0]
    square = lax.optimization_barrier(jnp.sum(displace * displace, axis=0))
    radius = jnp.sqrt(square + SOFTENING)
    direction = displace / radius
    cutoff = jnp.where(square < CUTOFF_SQUARE, (1.0 - square / CUTOFF_SQUARE) ** 2, 0.0)
    centres = 0.5 + (CUTOFF_RADIUS - 0.5) * jnp.arange(basis_count, dtype=jnp.float32) / (basis_count - 1)
    radial = jnp.exp(-BASIS_SHARPNESS * (radius[:, :, None] - centres) ** 2).reshape(-1, basis_count)
    latent = jax.nn.silu(jnp.dot(radial, w_radial, precision=lax.Precision.HIGHEST)) * cutoff.reshape(-1, 1)
    latent_half = latent.astype(jnp.bfloat16)
    values = jnp.dot(latent_half, w_env, preferred_element_type=jnp.float32).reshape(neighbour_count, row_count, width)
    moment = jnp.einsum('anr,nrf->arf', direction, values, precision=lax.Precision.HIGHEST)
    invariant = jnp.einsum('arf,anr->nrf', moment, direction, precision=lax.Precision.HIGHEST).astype(jnp.bfloat16)
    joined = jnp.concatenate([latent_half, invariant.reshape(-1, width)], axis=1)
    hidden = jax.nn.silu(jnp.dot(joined, w_latent, preferred_element_type=jnp.float32)).astype(jnp.bfloat16)
    edge = jnp.dot(hidden, w_out, preferred_element_type=jnp.float32).reshape(neighbour_count, row_count) * cutoff
    return lax.optimization_barrier(jnp.sum(edge, axis=0))

def energies_and_grads(displace, weights):
    energy, pullback = jax.vjp(lambda piece: site_energy(piece, *weights), displace)
    return (energy, pullback(jnp.ones_like(energy))[0])

def reference(positions, velocities, forces_in, counts, neighbours, send_list, w_radial, w_env, w_latent, w_out):
    weights = (w_radial, w_env, w_latent, w_out)
    total = NX * NY * NZ * P_SIZE
    devices_all = N_GX * N_GY * N_GZ
    entry_codes = neighbours.reshape(NBR, NX, NY, NZ, P_SIZE)
    offset_code = entry_codes // P_SIZE
    slot_code = entry_codes % P_SIZE
    shift_x = offset_code // 9 - 1
    shift_y = offset_code // 3 % 3 - 1
    shift_z = offset_code % 3 - 1
    grid_x = jnp.arange(NX, dtype=jnp.int32).reshape(1, NX, 1, 1, 1)
    grid_y = jnp.arange(NY, dtype=jnp.int32).reshape(1, 1, NY, 1, 1)
    grid_z = jnp.arange(NZ, dtype=jnp.int32).reshape(1, 1, 1, NZ, 1)
    target_x = (grid_x + shift_x) % NX
    target_y = (grid_y + shift_y) % NY
    target_z = (grid_z + shift_z) % NZ
    neighbour_id = (((target_x * NY + target_y) * NZ + target_z) * P_SIZE + slot_code).reshape(NBR, total).astype(jnp.int32)
    shift = jnp.stack([shift_x, shift_y, shift_z]).astype(jnp.float32).reshape(3, NBR, total) * CELL_LENGTH
    occupied = (jnp.arange(P_SIZE, dtype=jnp.int32).reshape(1, 1, 1, P_SIZE) < counts[:, :, :, None]).reshape(total)
    usable = jnp.logical_and(occupied[None, :], occupied[neighbour_id])
    far_vector = jnp.array([FAR_OFFSET, 0.0, 0.0], dtype=jnp.float32).reshape(3, 1, 1)
    source_rows = send_list.reshape(N_GX, N_GY, N_GZ, N_GZ, CAP).transpose(0, 1, 3, 2, 4).reshape(devices_all, SLOTS)
    valid = source_rows >= 0
    local_slot = jnp.where(valid, source_rows, 0)
    device_index = jnp.arange(devices_all, dtype=jnp.int32).reshape(devices_all, 1)
    device_x = device_index // (N_GY * N_GZ)
    device_y = device_index // N_GZ % N_GY
    sender = (jnp.arange(SLOTS, dtype=jnp.int32) // CAP).reshape(1, SLOTS)
    cell_x = local_slot // (CY * CZ * P_SIZE)
    cell_y = local_slot // (CZ * P_SIZE) % CY
    cell_z = local_slot // P_SIZE % CZ
    within = local_slot % P_SIZE
    atom_id = (((device_x * CX + cell_x) * NY + device_y * CY + cell_y) * NZ + sender * CZ + cell_z) * P_SIZE + within
    order = jnp.argsort(jnp.where(valid, 0, 1), axis=1, stable=True)[:, :WORK].astype(jnp.int32)
    chosen = jnp.take_along_axis(atom_id, order, axis=1).astype(jnp.int32)

    def evaluate(coords):
        flat = coords.reshape(3, total)
        displace = flat[:, neighbour_id] - flat[:, None, :] + shift
        displace = jnp.where(usable[None], displace, far_vector)

        def one_device(identity):
            return energies_and_grads(displace[:, :, identity], weights)
        energy, grads = lax.map(one_device, chosen)
        work_energy = jnp.zeros((devices_all, SLOTS), jnp.float32).at[device_index, order].set(energy)
        per_atom = jnp.zeros((3, NBR, total), jnp.float32).at[:, :, chosen.reshape(-1)].set(grads.transpose(1, 2, 0, 3).reshape(3, NBR, -1))
        force = lax.optimization_barrier(jnp.sum(per_atom, axis=1))
        force = force.at[:, neighbour_id.reshape(-1)].add(-per_atom.reshape(3, -1))
        return (force.reshape(3, NX, NY, NZ * P_SIZE), work_energy.reshape(N_GX, N_GY, N_GZ * SLOTS))
    coords, speed, force = (positions, velocities, forces_in)
    work_energy = jnp.zeros((N_GX, N_GY, N_GZ * SLOTS), jnp.float32)
    for repeat in range(STEPS):
        speed = speed + 0.5 * TIME_STEP * force
        coords = coords + TIME_STEP * speed
        force, work_energy = evaluate(coords)
        speed = speed + 0.5 * TIME_STEP * force
    return (coords, speed, force, work_energy)
```

```python
import functools

import jax
import jax.numpy as jnp
from jax import lax
from jax.experimental import pallas as pl
from jax.experimental.pallas import tpu as pltpu
from jax.sharding import PartitionSpec as P

STEPS = 2
TIME_STEP = 0.5
BASIS = 8
CENTRE_FIRST = 0.5
CENTRE_STEP = 1.5 / 7.0
UNOCCUPIED = 1e30
FAR = 3.0
F32 = jnp.float32
BF16 = jnp.bfloat16

CELLS = 16
ROWS = 8
USED = 6
TILES = 3


def dot(a, b):
    return lax.dot_general(a, b, (((1,), (0,)), ((), ())), preferred_element_type=F32)


def dot_nt(a, b):
    return lax.dot_general(a, b, (((1,), (1,)), ((), ())), preferred_element_type=F32)


def pair_row(block, t):
    return jnp.concatenate([block[2 * t : 2 * t + 1], block[2 * t + 1 : 2 * t + 2]], axis=1)


def force_kernel(
    tab_ref,
    key_ref,
    wr_ref,
    wrb_ref,
    wtf_ref,
    wtop_ref,
    webf_ref,
    web_ref,
    wo_ref,
    spread_ref,
    energy_ref,
    geo,
    res,
    work,
    slope,
    acc,
):
    lane32 = lax.broadcasted_iota(jnp.int32, (32, 128), 1)
    row32 = lax.broadcasted_iota(jnp.int32, (32, 128), 0)
    for block in range(4):
        cx, cy = block // 2, block % 2
        rows = slice(32 * block, 32 * block + 32)
        key = key_ref[rows, :]
        col = key >> 8
        place = key & 255
        low = place & 127
        upper = place >= 128
        own_place = 32 * (row32 // ROWS + 1) + lane32 % 32
        own_low = own_place & 127
        own_upper = own_place >= 128
        own = []
        other = []
        for a in range(3):
            found = None
            for ox in range(3):
                for oy in range(3):
                    c = (cx + ox) * 4 + cy + oy
                    line = a * 16 + c
                    first = jnp.broadcast_to(tab_ref[line : line + 1, 0:128], (32, 128))
                    second = jnp.broadcast_to(tab_ref[line : line + 1, 128:256], (32, 128))
                    picked = jnp.where(
                        upper,
                        jnp.take_along_axis(second, low, axis=1, mode="promise_in_bounds"),
                        jnp.take_along_axis(first, low, axis=1, mode="promise_in_bounds"),
                    )
                    found = picked if found is None else jnp.where(col == c, picked, found)
                    if ox == 1 and oy == 1:
                        own.append(
                            jnp.where(
                                own_upper,
                                jnp.take_along_axis(
                                    second, own_low, axis=1, mode="promise_in_bounds"
                                ),
                                jnp.take_along_axis(
                                    first, own_low, axis=1, mode="promise_in_bounds"
                                ),
                            )
                        )
            other.append(found)
        usable = jnp.logical_and(own[0] < 0.5 * UNOCCUPIED, other[0] < 0.5 * UNOCCUPIED)
        shift = (
            (col >> 2) - (cx + 1),
            (col & 3) - (cy + 1),
            (place >> 5) - (row32 // ROWS + 1),
        )
        far = (FAR, 0.0, 0.0)
        displace = [
            jnp.where(usable, other[a] - own[a] + shift[a].astype(F32), far[a]) for a in range(3)
        ]
        square = displace[0] ** 2 + displace[1] ** 2 + displace[2] ** 2
        radius = jnp.sqrt(square + 0.25)
        inverse = 1.0 / radius
        geo[0, rows, :] = radius
        geo[1, rows, :] = jnp.maximum(1.0 - 0.25 * square, 0.0)
        for a in range(3):
            geo[2 + a, rows, :] = displace[a] * inverse
            geo[5 + a, rows, :] = displace[a]

    same = lax.broadcasted_iota(jnp.int32, (32, 256), 1) % 32 == lax.broadcasted_iota(
        jnp.int32, (32, 256), 0
    )
    centre = CENTRE_FIRST + CENTRE_STEP * lax.broadcasted_iota(jnp.int32, (BASIS, 256), 0).astype(
        F32
    )

    def one_cell(cell):
        start = pl.multiple_of(cell * ROWS, ROWS)
        radius8 = geo[0, pl.ds(start, ROWS), :]
        root8 = geo[1, pl.ds(start, ROWS), :]
        dir8 = [geo[2 + a, pl.ds(start, ROWS), :] for a in range(3)]
        for t in range(TILES):
            lanes = slice(256 * t, 256 * t + 256)
            away = pair_row(radius8, t) - centre
            radial = jnp.exp(-4.0 * away * away)
            high = radial.astype(BF16).astype(F32)
            stacked = jnp.concatenate(
                [high, radial - high, high, jnp.zeros_like(high)], axis=0
            ).astype(BF16)
            zh = dot(wr_ref[...], stacked)
            th = jnp.tanh(zh)
            up = 1.0 + th
            root = pair_row(root8, t)
            work[0:128, lanes] = (zh * up * (root * root)).astype(BF16)
            slope[:, lanes] = up * (1.0 + zh * (1.0 - th))
            for a in range(3):
                work[128 + 32 * a : 160 + 32 * a, lanes] = jnp.where(
                    same, pair_row(dir8[a], t), 0.0
                ).astype(BF16)
            work[224:256, lanes] = jnp.zeros((32, 256), BF16)
        gathered = dot_nt(work[0:128, :], work[128:256, :])
        mixed = dot(webf_ref[...], gathered.astype(BF16))
        mixed_t = (2.0 * mixed.T).astype(BF16)
        left = jnp.concatenate([wtf_ref[...], mixed.astype(BF16)], axis=1)
        for t in range(TILES):
            lanes = slice(256 * t, 256 * t + 256)
            ph = dot(left, work[0:256, lanes])
            th = jnp.tanh(ph)
            up = 1.0 + th
            root = pair_row(root8, t)
            readout = wo_ref[...]
            energy = jnp.sum(readout * (ph * up), axis=0, keepdims=True)
            res[4, pl.ds(start + 2 * t, 1), :] = energy[:, 0:128]
            res[4, pl.ds(start + 2 * t + 1, 1), :] = energy[:, 128:256]
            work[256:384, lanes] = (
                (readout * (0.5 * root * root)) * (up * (1.0 + ph * (1.0 - th)))
            ).astype(BF16)
        back = dot_nt(work[256:384, :], work[128:256, :])
        back = dot(web_ref[...], back.astype(BF16))
        back_t = back.T.astype(BF16)
        left = jnp.concatenate([back.astype(BF16), wtop_ref[...]], axis=1)
        for t in range(TILES):
            lanes = slice(256 * t, 256 * t + 256)
            latent = work[0:128, lanes]
            slant = dot(left, work[128:384, lanes])
            turned = dot(mixed_t, work[256:384, lanes]) + dot(back_t, latent)
            outcome = [
                jnp.sum(jnp.where(same, turned[32 * a : 32 * a + 32], 0.0), axis=0, keepdims=True)
                for a in range(3)
            ]
            outcome.append(jnp.sum(slant * latent.astype(F32), axis=0, keepdims=True))
            basis_grad = dot(wrb_ref[...], (slant * slope[:, lanes]).astype(BF16))
            away = pair_row(radius8, t) - centre
            radial = jnp.exp(-4.0 * away * away) * (-8.0 * away)
            outcome.append(
                jnp.sum(
                    (basis_grad[0:BASIS] + basis_grad[BASIS : 2 * BASIS]) * radial,
                    axis=0,
                    keepdims=True,
                )
            )
            for value, slot in zip(outcome, (0, 1, 2, 3, 5)):
                res[slot, pl.ds(start + 2 * t, 1), :] = value[:, 0:128]
                res[slot, pl.ds(start + 2 * t + 1, 1), :] = value[:, 128:256]

    pl.loop(0, CELLS)(one_cell)

    for block in range(4):
        rows = slice(32 * block, 32 * block + 32)
        radius = geo[0, rows, :]
        root = geo[1, rows, :]
        inverse = 1.0 / radius
        cutoff = root * root
        readout = res[4, rows, :]
        live = root > 0.0
        root_inverse = jnp.where(live, 1.0 / jnp.where(live, root, 1.0), 0.0)
        along = res[5, rows, :] * cutoff
        for a in range(3):
            along = along - res[a, rows, :] * geo[2 + a, rows, :] * inverse
        to_square = along * (0.5 * inverse) - 0.5 * (
            root * readout + root_inverse * res[3, rows, :]
        )
        for a in range(3):
            geo[2 + a, rows, :] = (
                res[a, rows, :] * inverse + geo[5 + a, rows, :] * (2.0 * to_square)
            )
        res[4, rows, :] = cutoff * readout

    acc[...] = jnp.zeros_like(acc)
    iota96 = lax.broadcasted_iota(jnp.int32, (96, 128), 0)
    lane96 = lax.broadcasted_iota(jnp.int32, (96, 128), 1)
    iota16 = lax.broadcasted_iota(jnp.int32, (16, 128), 0)
    own_hot = jnp.where(iota96 == 32 + lane96 % 32, 1.0, 0.0).astype(BF16)

    def spread_rows(col_row, terms):
        highs, lows = [], []
        for term in terms:
            chosen = jnp.where(col_row == iota16, term, 0.0)
            high = chosen.astype(BF16)
            highs.append(high)
            lows.append((chosen - high.astype(F32)).astype(BF16))
        return jnp.concatenate(highs + lows, axis=0)

    def scatter_cell(cell):
        start = pl.multiple_of(cell * ROWS, ROWS)
        block, cz = cell // 4, cell % 4
        own_col = (block // 2 + 1) * 4 + block % 2 + 1
        key = key_ref[pl.ds(start, ROWS), :]
        col = key >> 8
        place = (key & 255) - 32 * cz
        term = [geo[2 + a, pl.ds(start, ROWS), :] for a in range(3)]
        hots, lefts = [own_hot], []
        sums = [jnp.sum(term[a][0:USED], axis=0, keepdims=True) for a in range(3)]
        lefts.append(spread_rows(own_col, sums))
        for r in range(USED):
            hots.append(jnp.where(iota96 == place[r : r + 1], 1.0, 0.0).astype(BF16))
            lefts.append(spread_rows(col[r : r + 1], [-term[a][r : r + 1] for a in range(3)]))
        added = dot_nt(jnp.concatenate(hots, axis=1), jnp.concatenate(lefts, axis=1))
        at = pl.multiple_of(cz * 32, 32)
        acc[pl.ds(at, 96), 0:96] += added
        energy = res[4, pl.ds(start, ROWS), :]
        energy_ref[pl.ds(cell, 1), :] = jnp.sum(energy[0:USED], axis=0, keepdims=True)

    pl.loop(0, CELLS)(scatter_cell)
    flipped = acc[...].T
    spread_ref[...] = flipped[0:48] + flipped[48:96]


def force_call(tab, key, weights):
    return pl.pallas_call(
        force_kernel,
        out_shape=(
            jax.ShapeDtypeStruct((48, 256), F32),
            jax.ShapeDtypeStruct((CELLS, 128), F32),
        ),
        scratch_shapes=[
            pltpu.VMEM((8, 128, 128), F32),
            pltpu.VMEM((6, 128, 128), F32),
            pltpu.VMEM((384, 768), BF16),
            pltpu.VMEM((128, 768), F32),
            pltpu.VMEM((256, 128), F32),
        ],
        compiler_params=pltpu.CompilerParams(vmem_limit_bytes=32 * 1024 * 1024),
        name="force",
    )(tab, key, *weights)


def prepare_weights(w_radial, w_env, w_latent, w_out):
    top = w_latent[0:128]
    both = jnp.dot(
        w_env.astype(F32), w_latent[128:256].astype(F32), precision=lax.Precision.HIGHEST
    )
    high = w_radial.astype(BF16)
    low = (w_radial - high.astype(F32)).astype(BF16)
    half = BF16(0.5)
    wr = jnp.concatenate([high, high, low, jnp.zeros_like(low)], axis=0).T * half
    wrb = jnp.concatenate([high, low], axis=0) * half
    wo = jnp.broadcast_to(w_out.astype(F32)[:, None], (128, 256))
    return (wr, wrb, top.T * half, top, (0.5 * both).T.astype(BF16), both.astype(BF16), wo)


def neighbour_keys(neighbours):
    code = neighbours.reshape(4, 6, 2, 2, 4, 32)
    offset = code // 32
    slot = code % 32
    grid = lambda n, dim: jnp.arange(n, dtype=jnp.int32).reshape(
        tuple(n if d == dim else 1 for d in range(6))
    )
    col = (grid(2, 2) + offset // 9) * 4 + grid(2, 3) + offset // 3 % 3
    place = (grid(4, 4) + offset % 3) * 32 + slot
    key = (col * 256 + place).transpose(2, 3, 4, 1, 0, 5).reshape(CELLS, USED, 128)
    return jnp.pad(key, ((0, 0), (0, ROWS - USED), (0, 0))).reshape(CELLS * ROWS, 128)


def with_halo(array, sides):
    for axis, dim in sides:
        peers, length = (lax.axis_size(axis), array.shape[dim])
        up = [(i, (i + 1) % peers) for i in range(peers)]
        down = [(j, i) for i, j in up]
        last = lax.slice_in_dim(array, length - 1, length, axis=dim)
        leading = lax.slice_in_dim(array, 0, 1, axis=dim)
        before = lax.ppermute(last, axis, up)
        after = lax.ppermute(leading, axis, down)
        array = jnp.concatenate([before, array, after], axis=dim)
    return array


def fold(spread, axis, dim):
    peers, length = (lax.axis_size(axis), spread.shape[dim])
    up = [(i, (i + 1) % peers) for i in range(peers)]
    down = [(j, i) for i, j in up]
    lower = lax.slice_in_dim(spread, 0, 1, axis=dim)
    upper = lax.slice_in_dim(spread, length - 1, length, axis=dim)
    from_below = lax.ppermute(upper, axis, up)
    from_above = lax.ppermute(lower, axis, down)
    inner = lax.slice_in_dim(spread, 1, length - 1, axis=dim)
    low_pad = [(0, 0, 0)] * spread.ndim
    low_pad[dim] = (0, length - 3, 0)
    high_pad = [(0, 0, 0)] * spread.ndim
    high_pad[dim] = (length - 3, 0, 0)
    zero = jnp.zeros((), spread.dtype)
    return inner + lax.pad(from_below, zero, low_pad) + lax.pad(from_above, zero, high_pad)


def on_device(
    positions,
    velocities,
    forces_in,
    counts,
    neighbours,
    send_list,
    w_radial,
    w_env,
    w_latent,
    w_out,
):
    weights = prepare_weights(w_radial, w_env, w_latent, w_out)
    key = neighbour_keys(neighbours)
    occupied = jnp.arange(32, dtype=jnp.int32).reshape(1, 1, 1, 32) < counts[:, :, :, None]
    coords, speed, force = (positions, velocities, forces_in)
    for repeat in range(STEPS):
        speed = speed + 0.5 * TIME_STEP * force
        coords = coords + TIME_STEP * speed
        masked = jnp.where(occupied[None], coords.reshape(3, 2, 2, 4, 32), UNOCCUPIED)
        padded = with_halo(masked, (("gx", 1), ("gy", 2), ("gz", 3)))
        tab = jnp.pad(padded.reshape(48, 192), ((0, 0), (0, 64)))
        spread, energy = force_call(tab, key, weights)
        spread = spread[:, 0:192].reshape(3, 4, 4, 6, 32)
        for axis, dim in (("gx", 1), ("gy", 2), ("gz", 3)):
            spread = fold(spread, axis, dim)
        force = spread.reshape(positions.shape)
        speed = speed + 0.5 * TIME_STEP * force
    site = jnp.sum(energy.reshape(CELLS, 4, 32), axis=1).reshape(512)
    listed = send_list.reshape(512)
    hot = (listed[None, :] == jnp.arange(512, dtype=jnp.int32)[:, None]).astype(F32)
    sent = jnp.dot(site.reshape(1, 512), hot, precision=lax.Precision.HIGHEST).reshape(16, 32)
    work_energy = lax.all_to_all(sent, "gz", split_axis=0, concat_axis=0, tiled=True)
    return (coords, speed, force, work_energy.reshape(1, 1, 512))


def solution(mesh):
    split = P(None, "gx", "gy", "gz")
    cells = P("gx", "gy", "gz")
    return jax.shard_map(
        on_device,
        mesh=mesh,
        in_specs=(split, split, split, cells, split, cells, P(), P(), P(), P()),
        out_specs=(split, split, split, cells),
        check_vma=False,
    )
```

```python
import functools

import jax
import jax.numpy as jnp
from jax import lax
from jax.experimental import pallas as pl
from jax.experimental.pallas import tpu as pltpu
from jax.sharding import PartitionSpec as P

STEPS = 2
TIME_STEP = 0.5
BASIS = 8
CENTRE_FIRST = 0.5
CENTRE_STEP = 1.5 / 7.0
UNOCCUPIED = 1e30
FAR = 3.0
F32 = jnp.float32
BF16 = jnp.bfloat16

CELLS = 16
ROWS = 8
USED = 6
TILES = 3


def dot(a, b):
    return lax.dot_general(a, b, (((1,), (0,)), ((), ())), preferred_element_type=F32)


def dot_nt(a, b):
    return lax.dot_general(a, b, (((1,), (1,)), ((), ())), preferred_element_type=F32)


def pair_row(block, t):
    return jnp.concatenate([block[2 * t : 2 * t + 1], block[2 * t + 1 : 2 * t + 2]], axis=1)


def lane_pick(line, place, shape):
    found = None
    for chunk in range(line.shape[1] // 128):
        table = jnp.broadcast_to(line[:, 128 * chunk : 128 * chunk + 128], shape)
        picked = jnp.take_along_axis(table, place & 127, axis=1, mode="promise_in_bounds")
        found = picked if found is None else jnp.where(place >= 128 * chunk, picked, found)
    return found


def force_kernel(blocks, layers, outer, first, last, *refs):
    refs = list(refs)
    tab_ref, key_ref = refs[:2]
    wr_ref, wtf_ref, wtop_ref, webf_ref, web_ref, wo_ref = refs[2:8]
    refs = refs[8:]
    if not first:
        before_ref, site_before_ref = refs[:2]
        refs = refs[2:]
    if last:
        list_ref = refs.pop(0)
    spread_ref, site_ref = refs[:2]
    refs = refs[2:]
    if outer:
        rim_ref = refs.pop(0)
    if last:
        sent_ref = refs.pop(0)
    geo, res, acc = refs[:3]
    cells = [(block, layer) for block in blocks for layer in layers]
    count = len(cells)
    works, slopes = refs[3 : 3 + count], refs[3 + count :]
    base = 0 if outer else 32
    shape = (2 * ROWS, 128)
    lane = lax.broadcasted_iota(jnp.int32, shape, 1)
    layer_of = layers[0] + (layers[1] - layers[0]) * (
        lax.broadcasted_iota(jnp.int32, shape, 0) // ROWS
    )
    own_place = 32 * (layer_of + 1) - base + lane % 32
    for number, block in enumerate(blocks):
        cx, cy = block // 2, block % 2
        rows = slice(2 * ROWS * number, 2 * ROWS * (number + 1))
        key = jnp.concatenate(
            [key_ref[(block * 4 + layer) * ROWS : (block * 4 + layer + 1) * ROWS] for layer in layers],
            axis=0,
        )
        col = key >> 8
        place = (key & 255) - base
        own = []
        other = []
        for a in range(3):
            found = None
            for ox in range(3):
                for oy in range(3):
                    c = (cx + ox) * 4 + cy + oy
                    line = tab_ref[a * 16 + c : a * 16 + c + 1, :]
                    picked = lane_pick(line, place, shape)
                    found = picked if found is None else jnp.where(col == c, picked, found)
                    if ox == 1 and oy == 1:
                        own.append(lane_pick(line, own_place, shape))
            other.append(found)
        usable = jnp.logical_and(own[0] < 0.5 * UNOCCUPIED, other[0] < 0.5 * UNOCCUPIED)
        shift = (
            (col >> 2) - (cx + 1),
            (col & 3) - (cy + 1),
            (place + base) // 32 - (layer_of + 1),
        )
        far = (FAR, 0.0, 0.0)
        displace = [
            jnp.where(usable, other[a] - own[a] + shift[a].astype(F32), far[a]) for a in range(3)
        ]
        square = displace[0] ** 2 + displace[1] ** 2 + displace[2] ** 2
        radius = jnp.sqrt(square + 0.25)
        inverse = 1.0 / radius
        root = jnp.maximum(1.0 - 0.25 * square, 0.0)
        geo[0, rows, :] = radius
        geo[1, rows, :] = root
        geo[8, rows, :] = -4.0 * inverse * (root * root)
        for a in range(3):
            geo[2 + a, rows, :] = displace[a] * inverse
            geo[5 + a, rows, :] = displace[a]

    same = lax.broadcasted_iota(jnp.int32, (32, 256), 1) % 32 == lax.broadcasted_iota(
        jnp.int32, (32, 256), 0
    )
    centre = CENTRE_FIRST + CENTRE_STEP * lax.broadcasted_iota(jnp.int32, (BASIS, 256), 0).astype(
        F32
    )

    def one_cell(cell, work, slope):
        start = cell * ROWS
        radius8 = geo[0, start : start + ROWS, :]
        root8 = geo[1, start : start + ROWS, :]
        scale8 = geo[8, start : start + ROWS, :]
        dir8 = [geo[2 + a, start : start + ROWS, :] for a in range(3)]
        for t in range(TILES):
            lanes = slice(256 * t, 256 * t + 256)
            away = pair_row(radius8, t) - centre
            radial = jnp.exp(-4.0 * away * away)
            steep = radial * (away * pair_row(scale8, t))
            high = radial.astype(BF16).astype(F32)
            steep_high = steep.astype(BF16).astype(F32)
            zero = jnp.zeros_like(high)
            stacked = jnp.concatenate(
                [high, radial - high, high, zero, steep_high, steep - steep_high, steep_high, zero],
                axis=0,
            ).astype(BF16)
            both = dot(wr_ref[...], stacked)
            zh = both[0:128]
            th = jnp.tanh(zh)
            up = 1.0 + th
            root = pair_row(root8, t)
            work[0:128, lanes] = (zh * up * (root * root)).astype(BF16)
            slope[:, lanes] = up * (
                (1.0 + zh * (1.0 - th)) * both[128:256] - zh * (0.5 * root)
            )
            for a in range(3):
                work[128 + 32 * a : 160 + 32 * a, lanes] = jnp.where(
                    same, pair_row(dir8[a], t), 0.0
                ).astype(BF16)
            work[224:256, lanes] = jnp.zeros((32, 256), BF16)
        yield
        gathered = dot_nt(work[0:128, :], work[128:256, :])
        mixed = dot(webf_ref[...], gathered.astype(BF16))
        mixed_t = (2.0 * mixed.T).astype(BF16)
        left = jnp.concatenate([wtf_ref[...], mixed.astype(BF16)], axis=1)
        yield
        for t in range(TILES):
            lanes = slice(256 * t, 256 * t + 256)
            ph = dot(left, work[0:256, lanes])
            th = jnp.tanh(ph)
            up = 1.0 + th
            root = pair_row(root8, t)
            readout = wo_ref[...]
            energy = jnp.sum(readout * (ph * up), axis=0, keepdims=True)
            res[4, start + 2 * t : start + 2 * t + 1, :] = energy[:, 0:128]
            res[4, start + 2 * t + 1 : start + 2 * t + 2, :] = energy[:, 128:256]
            work[256:384, lanes] = (
                (readout * (0.5 * root * root)) * (up * (1.0 + ph * (1.0 - th)))
            ).astype(BF16)
        yield
        back = dot_nt(work[256:384, :], work[128:256, :])
        back = dot(web_ref[...], back.astype(BF16))
        back_t = back.T.astype(BF16)
        left = jnp.concatenate(
            [
                jnp.concatenate([back.astype(BF16), wtop_ref[...]], axis=1),
                jnp.concatenate([jnp.zeros((96, 128), BF16), mixed_t[0:96]], axis=1),
            ],
            axis=0,
        )
        yield
        for t in range(TILES):
            lanes = slice(256 * t, 256 * t + 256)
            latent = work[0:128, lanes]
            slant = dot(left, work[128:384, lanes])
            turned = slant[128:224] + dot(back_t[0:96], latent)
            outcome = [
                jnp.sum(jnp.where(same, turned[32 * a : 32 * a + 32], 0.0), axis=0, keepdims=True)
                for a in range(3)
            ]
            outcome.append(jnp.sum(slant[0:128] * slope[:, lanes], axis=0, keepdims=True))
            for value, slot in zip(outcome, (0, 1, 2, 3)):
                res[slot, start + 2 * t : start + 2 * t + 1, :] = value[:, 0:128]
                res[slot, start + 2 * t + 1 : start + 2 * t + 2, :] = value[:, 128:256]

    runs = [one_cell(k, works[k], slopes[k]) for k in range(count)]
    done = object()
    for tick in range(6 + count):
        for k in range(count):
            if tick >= k and runs[k] is not None:
                if next(runs[k], done) is done:
                    runs[k] = None

    for number in range(len(blocks)):
        rows = slice(2 * ROWS * number, 2 * ROWS * (number + 1))
        radius = geo[0, rows, :]
        root = geo[1, rows, :]
        inverse = 1.0 / radius
        readout = res[4, rows, :]
        along = res[0, rows, :] * geo[2, rows, :]
        for a in range(1, 3):
            along = along + res[a, rows, :] * geo[2 + a, rows, :]
        to_square = res[3, rows, :] - 0.5 * (root * readout + inverse * inverse * along)
        for a in range(3):
            geo[2 + a, rows, :] = (
                res[a, rows, :] * inverse + geo[5 + a, rows, :] * (2.0 * to_square)
            )
        res[4, rows, :] = root * root * readout

    acc[...] = jnp.zeros_like(acc)
    iota96 = lax.broadcasted_iota(jnp.int32, (96, 128), 0)
    lane96 = lax.broadcasted_iota(jnp.int32, (96, 128), 1)
    iota16 = lax.broadcasted_iota(jnp.int32, (16, 128), 0)
    own_hot = jnp.where(iota96 == 32 + lane96 % 32, 1.0, 0.0).astype(BF16)

    def spread_rows(col_row, terms):
        highs, lows = [], []
        for term in terms:
            chosen = jnp.where(col_row == iota16, term, 0.0)
            high = chosen.astype(BF16)
            highs.append(high)
            lows.append((chosen - high.astype(F32)).astype(BF16))
        return jnp.concatenate(highs + lows, axis=0)

    site = [jnp.zeros((1, 128), F32) for _ in range(4)]
    lane1 = lax.broadcasted_iota(jnp.int32, (1, 128), 1)
    for k, (block, layer) in enumerate(cells):
        start = k * ROWS
        own_col = (block // 2 + 1) * 4 + block % 2 + 1
        key = key_ref[(block * 4 + layer) * ROWS : (block * 4 + layer + 1) * ROWS]
        col = key >> 8
        place = (key & 255) - 32 * layer
        term = [geo[2 + a, start : start + ROWS, :] for a in range(3)]
        hots, lefts = [own_hot], []
        sums = [jnp.sum(term[a][0:USED], axis=0, keepdims=True) for a in range(3)]
        lefts.append(spread_rows(own_col, sums))
        for r in range(USED):
            hots.append(jnp.where(iota96 == place[r : r + 1], 1.0, 0.0).astype(BF16))
            lefts.append(spread_rows(col[r : r + 1], [-term[a][r : r + 1] for a in range(3)]))
        added = dot_nt(jnp.concatenate(hots, axis=1), jnp.concatenate(lefts, axis=1))
        at = 32 * layer - base
        acc[at : at + 96, 0:96] += added
        energy = jnp.sum(res[4, start : start + USED, :], axis=0, keepdims=True)
        energy = energy + pltpu.roll(energy, 32, 1)
        energy = energy + pltpu.roll(energy, 64, 1)
        site[block] = jnp.where(lane1 // 32 == layer, energy, site[block])

    flipped = acc[32 - base : 160 - base, :].T
    total = flipped[0:48] + flipped[48:96]
    site = jnp.concatenate(site + [jnp.zeros((4, 128), F32)], axis=0)
    if not first:
        total = total + before_ref[...]
        site = site + site_before_ref[...]
    spread_ref[...] = total
    site_ref[...] = site
    if outer:
        edge = jnp.concatenate([acc[0:32, :], acc[160:192, :], jnp.zeros((64, 128), F32)], axis=0).T
        rim_ref[...] = edge[0:48] + edge[48:96]
    if last:
        listed = list_ref[...]
        sent = jnp.zeros((16, 128), F32)
        for block in range(4):
            table = jnp.broadcast_to(site[block : block + 1], (16, 128))
            picked = jnp.take_along_axis(table, listed & 127, axis=1, mode="promise_in_bounds")
            sent = jnp.where(listed >> 7 == block, picked, sent)
        sent_ref[...] = sent


def force_call(tab, key, weights, blocks, layers, before=None, listed=None):
    outer = tab.shape[1] == 256
    first, last = before is None, listed is not None
    count = 2 * len(blocks)
    args = [tab, key, *weights]
    if not first:
        args += list(before)
    if last:
        args.append(listed)
    outs = [jax.ShapeDtypeStruct((48, 128), F32), jax.ShapeDtypeStruct((8, 128), F32)]
    if outer:
        outs.append(jax.ShapeDtypeStruct((48, 128), F32))
    if last:
        outs.append(jax.ShapeDtypeStruct((16, 128), F32))
    return pl.pallas_call(
        functools.partial(force_kernel, blocks, layers, outer, first, last),
        out_shape=tuple(outs),
        scratch_shapes=[
            pltpu.VMEM((9, count * ROWS, 128), F32),
            pltpu.VMEM((5, count * ROWS, 128), F32),
            pltpu.VMEM((192 if outer else 128, 128), F32),
        ]
        + [pltpu.VMEM((384, 768), BF16)] * count
        + [pltpu.VMEM((128, 768), F32)] * count,
        compiler_params=pltpu.CompilerParams(vmem_limit_bytes=40 * 1024 * 1024),
        cost_estimate=pl.CostEstimate(
            flops=count * 800_000_000, bytes_accessed=300_000, transcendentals=0
        ),
        name="force",
    )(*args)


def energy_rows_kernel(in_ref, out_ref):
    lane = lax.broadcasted_iota(jnp.int32, (1, 128), 1)
    for row in range(4):
        line = in_ref[4 * row : 4 * row + 1, :]
        for part in range(1, 4):
            moved = pltpu.roll(in_ref[4 * row + part : 4 * row + part + 1, :], 32 * part, 1)
            line = jnp.where(lane // 32 == part, moved, line)
        out_ref[row : row + 1, :] = line


def prepare_weights(w_radial, w_env, w_latent, w_out):
    top = w_latent[0:128]
    both = jnp.dot(
        w_env.astype(F32), w_latent[128:256].astype(F32), precision=lax.Precision.HIGHEST
    )
    high = w_radial.astype(BF16)
    low = (w_radial - high.astype(F32)).astype(BF16)
    half = BF16(0.5)
    wr = jnp.concatenate([high, high, low, jnp.zeros_like(low)], axis=0).T * half
    wr = jnp.concatenate([jnp.pad(wr, ((0, 0), (0, 32))), jnp.pad(wr, ((0, 0), (32, 0)))], axis=0)
    wo = jnp.broadcast_to(w_out.astype(F32)[:, None], (128, 256))
    return (wr, top.T * half, top, (0.5 * both).T.astype(BF16), both.astype(BF16), wo)


def neighbour_keys(neighbours):
    code = neighbours.reshape(4, 6, 2, 2, 4, 32)
    offset = code // 32
    slot = code % 32
    grid = lambda n, dim: jnp.arange(n, dtype=jnp.int32).reshape(
        tuple(n if d == dim else 1 for d in range(6))
    )
    col = (grid(2, 2) + offset // 9) * 4 + grid(2, 3) + offset // 3 % 3
    place = (grid(4, 4) + offset % 3) * 32 + slot
    key = (col * 256 + place).transpose(2, 3, 4, 1, 0, 5).reshape(CELLS, USED, 128)
    return jnp.pad(key, ((0, 0), (0, ROWS - USED), (0, 0))).reshape(CELLS * ROWS, 128)


def both_ways(array, axis, dim, low, high):
    peers = lax.axis_size(axis)
    up = [(i, (i + 1) % peers) for i in range(peers)]
    down = [(j, i) for i, j in up]
    from_below = lax.ppermute(lax.slice_in_dim(array, *high, axis=dim), axis, up)
    from_above = lax.ppermute(lax.slice_in_dim(array, *low, axis=dim), axis, down)
    return from_below, from_above


def with_halo(array, axis, dim):
    length = array.shape[dim]
    below, above = both_ways(array, axis, dim, (0, 1), (length - 1, length))
    return jnp.concatenate([below, array, above], axis=dim)


def share(padded, axis, dim):
    below, above = both_ways(padded, axis, dim, (0, 2), (2, 4))
    return padded + jnp.concatenate([below, above], axis=dim)


def fold(padded, axis, dim):
    below, above = both_ways(padded, axis, dim, (0, 1), (3, 4))
    return lax.slice_in_dim(padded, 1, 3, axis=dim) + jnp.concatenate([below, above], axis=dim)


def on_device(
    positions,
    velocities,
    forces_in,
    counts,
    neighbours,
    send_list,
    w_radial,
    w_env,
    w_latent,
    w_out,
):
    weights = prepare_weights(w_radial, w_env, w_latent, w_out)
    key = neighbour_keys(neighbours)
    listed = jnp.pad(send_list.reshape(16, 32), ((0, 0), (0, 96)))
    occupied = jnp.arange(32, dtype=jnp.int32).reshape(1, 1, 1, 32) < counts[:, :, :, None]
    occupied = occupied.reshape(1, 2, 2, 128)
    half, quarter = TIME_STEP, 0.5 * TIME_STEP
    speed = velocities + quarter * forces_in
    coords = positions + half * speed
    wide = jnp.concatenate([jnp.where(occupied, coords, UNOCCUPIED), speed], axis=0)
    wide = with_halo(with_halo(wide, "gx", 1), "gy", 2)
    wide_coords, wide_speed = wide[0:3], wide[3:6]
    for repeat in range(STEPS):
        final = repeat == STEPS - 1
        below, above = both_ways(wide_coords, "gz", 3, (0, 32), (96, 128))
        flat = wide_coords.reshape(48, 128)
        state = force_call(flat, key, weights, (0, 1), (1, 2))
        tab = jnp.concatenate(
            [below.reshape(48, 32), flat, above.reshape(48, 32), jnp.zeros((48, 64), F32)], axis=1
        )
        *state, rim = force_call(tab, key, weights, (0, 1, 2, 3), (0, 3), before=state)
        below, above = both_ways(rim.reshape(3, 4, 4, 128), "gz", 3, (0, 32), (32, 64))
        state = force_call(
            flat, key, weights, (2, 3), (1, 2), before=state, listed=listed if final else None
        )
        edges = jnp.concatenate([below, jnp.zeros((3, 4, 4, 64), F32), above], axis=3)
        force = state[0].reshape(3, 4, 4, 128) + edges
        if final:
            work_energy = lax.all_to_all(state[2], "gz", split_axis=0, concat_axis=0, tiled=True)
            force = fold(fold(force, "gx", 1), "gy", 2)
            speed = speed + quarter * force
        else:
            force = share(share(force, "gx", 1), "gy", 2)
            wide_speed = wide_speed + half * force
            wide_coords = wide_coords + half * wide_speed
            speed = speed + half * force[:, 1:3, 1:3]
            coords = coords + half * speed
    work_energy = pl.pallas_call(
        energy_rows_kernel, out_shape=jax.ShapeDtypeStruct((4, 128), F32), name="rows"
    )(work_energy)
    return (coords, speed, force, work_energy.reshape(1, 1, 512))


def solution(mesh):
    split = P(None, "gx", "gy", "gz")
    cells = P("gx", "gy", "gz")
    return jax.shard_map(
        on_device,
        mesh=mesh,
        in_specs=(split, split, split, cells, split, cells, P(), P(), P(), P()),
        out_specs=(split, split, split, cells),
        check_vma=False,
    )
```

```python
import functools

import jax
import jax.numpy as jnp
from jax import lax
from jax.experimental import pallas as pl
from jax.experimental.pallas import tpu as pltpu
from jax.sharding import PartitionSpec as P

STEPS = 2
TIME_STEP = 0.5
BASIS = 8
CENTRE_FIRST = 0.5
CENTRE_STEP = 1.5 / 7.0
UNOCCUPIED = 1e30
FAR = 3.0
F32 = jnp.float32
BF16 = jnp.bfloat16

CELLS = 16
ROWS = 8
USED = 6
TILES = 3


def dot(a, b):
    return lax.dot_general(a, b, (((1,), (0,)), ((), ())), preferred_element_type=F32)


def dot_nt(a, b):
    return lax.dot_general(a, b, (((1,), (1,)), ((), ())), preferred_element_type=F32)


def pair_row(block, t):
    return jnp.concatenate([block[2 * t : 2 * t + 1], block[2 * t + 1 : 2 * t + 2]], axis=1)


def lane_pick(line, place, shape):
    table = jnp.broadcast_to(line, shape)
    return jnp.take_along_axis(table, place, axis=1, mode="promise_in_bounds")


def force_kernel(blocks, layers, first, last, *refs):
    refs = list(refs)
    outer = len(layers) == 1
    base = layers[0] // 3 * 64 if outer else 32
    tab_ref, key_ref = refs[:2]
    wr_ref, wtf_ref, wtop_ref, webf_ref, web_ref, wo_ref = refs[2:8]
    refs = refs[8:]
    if outer:
        halo_ref = refs.pop(0)
    if not first:
        before_ref, site_before_ref = refs[:2]
        refs = refs[2:]
    if last:
        list_ref = refs.pop(0)
    spread_ref, site_ref, extra_ref = refs[:3]
    geo, res, acc, own_sum, table_ref = refs[3:8]
    cells = [(block, layer) for block in blocks for layer in layers]
    count = len(cells)
    works, slopes = refs[8 : 8 + count], refs[8 + count :]
    if outer:
        lane48 = lax.broadcasted_iota(jnp.int32, (48, 128), 1)
        halo = jnp.concatenate([halo_ref[...], jnp.zeros((48, 96), F32)], axis=1)
        if base == 0:
            table_ref[...] = jnp.where(lane48 < 32, halo, pltpu.roll(tab_ref[...], 32, 1))
        else:
            table_ref[...] = jnp.where(
                lane48 < 96, pltpu.roll(tab_ref[...], 96, 1), pltpu.roll(halo, 96, 1)
            )
    else:
        table_ref = tab_ref
    high = len(layers)
    shape = (high * ROWS, 128)
    lane = lax.broadcasted_iota(jnp.int32, shape, 1)
    layer_of = layers[0] + lax.broadcasted_iota(jnp.int32, shape, 0) // ROWS
    own_place = 32 * (layer_of + 1) - base + lane % 32
    for number, block in enumerate(blocks):
        cx, cy = block // 2, block % 2
        key = jnp.concatenate([key_ref[block, layer] for layer in layers], axis=0)
        col = key >> 8
        place = (key & 255) - base
        own = []
        other = []
        for a in range(3):
            found = None
            for ox in range(3):
                for oy in range(3):
                    c = (cx + ox) * 4 + cy + oy
                    line = table_ref[a * 16 + c : a * 16 + c + 1, :]
                    picked = lane_pick(line, place, shape)
                    found = picked if found is None else jnp.where(col == c, picked, found)
                    if ox == 1 and oy == 1:
                        own.append(lane_pick(line, own_place, shape))
            other.append(found)
        usable = jnp.logical_and(own[0] < 0.5 * UNOCCUPIED, other[0] < 0.5 * UNOCCUPIED)
        shift = (
            (col >> 2) - (cx + 1),
            (col & 3) - (cy + 1),
            (place + base) // 32 - (layer_of + 1),
        )
        far = (FAR, 0.0, 0.0)
        displace = [
            jnp.where(usable, other[a] - own[a] + shift[a].astype(F32), far[a]) for a in range(3)
        ]
        square = displace[0] ** 2 + displace[1] ** 2 + displace[2] ** 2
        radius = jnp.sqrt(square + 0.25)
        inverse = 1.0 / radius
        root = jnp.maximum(1.0 - 0.25 * square, 0.0)
        kept = [radius, root] + [displace[a] * inverse for a in range(3)] + displace
        kept.append(-4.0 * inverse * (root * root))
        for slot, value in enumerate(kept):
            for k in range(high):
                geo[slot, number * high + k] = value[ROWS * k : ROWS * k + ROWS]

    same = lax.broadcasted_iota(jnp.int32, (32, 256), 1) % 32 == lax.broadcasted_iota(
        jnp.int32, (32, 256), 0
    )
    centre = CENTRE_FIRST + CENTRE_STEP * lax.broadcasted_iota(jnp.int32, (BASIS, 256), 0).astype(
        F32
    )

    def one_cell(k, work, slope):
        radius8 = geo[0, k]
        root8 = geo[1, k]
        scale8 = geo[8, k]
        dir8 = [geo[2 + a, k] for a in range(3)]
        for t in range(TILES):
            lanes = slice(256 * t, 256 * t + 256)
            away = pair_row(radius8, t) - centre
            radial = jnp.exp(-4.0 * away * away)
            steep = radial * (away * pair_row(scale8, t))
            high = radial.astype(BF16).astype(F32)
            steep_high = steep.astype(BF16).astype(F32)
            zero = jnp.zeros_like(high)
            stacked = jnp.concatenate(
                [high, radial - high, high, zero, steep_high, steep - steep_high, steep_high, zero],
                axis=0,
            ).astype(BF16)
            both = dot(wr_ref[...], stacked)
            zh = both[0:128]
            th = jnp.tanh(zh)
            up = 1.0 + th
            root = pair_row(root8, t)
            work[0:128, lanes] = (zh * up * (root * root)).astype(BF16)
            slope[:, lanes] = up * (
                (1.0 + zh * (1.0 - th)) * both[128:256] - zh * (0.5 * root)
            )
            for a in range(3):
                work[128 + 32 * a : 160 + 32 * a, lanes] = jnp.where(
                    same, pair_row(dir8[a], t), 0.0
                ).astype(BF16)
            work[224:256, lanes] = jnp.zeros((32, 256), BF16)
        yield
        gathered = dot_nt(work[0:128, :], work[128:256, :])
        mixed = dot(webf_ref[...], gathered.astype(BF16))
        mixed_t = (2.0 * mixed.T).astype(BF16)
        left = jnp.concatenate([wtf_ref[...], mixed.astype(BF16)], axis=1)
        yield
        for t in range(TILES):
            lanes = slice(256 * t, 256 * t + 256)
            ph = dot(left, work[0:256, lanes])
            th = jnp.tanh(ph)
            up = 1.0 + th
            root = pair_row(root8, t)
            readout = wo_ref[...]
            energy = jnp.sum(readout * (ph * up), axis=0, keepdims=True)
            res[4, k, 2 * t : 2 * t + 1] = energy[:, 0:128]
            res[4, k, 2 * t + 1 : 2 * t + 2] = energy[:, 128:256]
            work[256:384, lanes] = (
                (readout * (0.5 * root * root)) * (up * (1.0 + ph * (1.0 - th)))
            ).astype(BF16)
        yield
        back = dot_nt(work[256:384, :], work[128:256, :])
        back = dot(web_ref[...], back.astype(BF16))
        back_t = back.T.astype(BF16)
        left = jnp.concatenate(
            [
                jnp.concatenate([back.astype(BF16), wtop_ref[...]], axis=1),
                jnp.concatenate([jnp.zeros((96, 128), BF16), mixed_t[0:96]], axis=1),
            ],
            axis=0,
        )
        yield
        for t in range(TILES):
            lanes = slice(256 * t, 256 * t + 256)
            latent = work[0:128, lanes]
            slant = dot(left, work[128:384, lanes])
            turned = slant[128:224] + dot(back_t[0:96], latent)
            outcome = [
                jnp.sum(jnp.where(same, turned[32 * a : 32 * a + 32], 0.0), axis=0, keepdims=True)
                for a in range(3)
            ]
            outcome.append(jnp.sum(slant[0:128] * slope[:, lanes], axis=0, keepdims=True))
            for value, slot in zip(outcome, (0, 1, 2, 3)):
                res[slot, k, 2 * t : 2 * t + 1] = value[:, 0:128]
                res[slot, k, 2 * t + 1 : 2 * t + 2] = value[:, 128:256]

    runs = [one_cell(k, works[k], slopes[k]) for k in range(count)]
    done = object()
    for tick in range(6 + count):
        for k in range(count):
            if tick >= k and runs[k] is not None:
                if next(runs[k], done) is done:
                    runs[k] = None

    radius, root = geo[0], geo[1]
    direction = [geo[2 + a] for a in range(3)]
    pull = [res[a] for a in range(3)]
    readout = res[4]
    inverse = 1.0 / radius
    along = pull[0] * direction[0] + pull[1] * direction[1] + pull[2] * direction[2]
    to_square = res[3] - 0.5 * (root * readout + inverse * inverse * along)
    for a in range(3):
        geo[2 + a] = pull[a] * inverse + geo[5 + a] * (2.0 * to_square)
    res[4] = root * root * readout

    acc[...] = jnp.zeros_like(acc)
    iota96 = lax.broadcasted_iota(jnp.int32, (96, 128), 0)
    iota16 = lax.broadcasted_iota(jnp.int32, (16, 128), 0)
    lane1 = lax.broadcasted_iota(jnp.int32, (1, 128), 1)
    own_sum[...] = jnp.zeros_like(own_sum)

    def spread_rows(col_row, terms):
        highs, lows = [], []
        for term in terms:
            chosen = jnp.where(col_row == iota16, term, 0.0)
            high = chosen.astype(BF16)
            highs.append(high)
            lows.append((chosen - high.astype(F32)).astype(BF16))
        return jnp.concatenate(highs + lows, axis=0)

    for k, (block, layer) in enumerate(cells):
        key = key_ref[block, layer]
        col = key >> 8
        place = (key & 255) - 32 * layer
        term = [geo[2 + a, k] for a in range(3)]
        hots, lefts = [], []
        for r in range(USED):
            hots.append(jnp.where(iota96 == place[r : r + 1], 1.0, 0.0).astype(BF16))
            lefts.append(spread_rows(col[r : r + 1], [-term[a][r : r + 1] for a in range(3)]))
        added = dot_nt(jnp.concatenate(hots, axis=1), jnp.concatenate(lefts, axis=1))
        at = 32 * layer - base
        acc[at : at + 96, 0:96] += added
        term.append(res[4, k])
        for slot in range(4):
            line = jnp.sum(term[slot][0:USED], axis=0, keepdims=True)
            line = line + pltpu.roll(line, 32, 1)
            line = line + pltpu.roll(line, 64, 1)
            own_sum[slot, block : block + 1, :] += jnp.where(lane1 // 32 == layer, line, 0.0)

    flipped = acc[...].T
    total = flipped[0:48] + flipped[48:96]
    if outer:
        extra_ref[...] = total
        turn, inside = (96, lane48 < 96) if base == 0 else (32, lane48 >= 32)
        total = jnp.where(inside, pltpu.roll(total, turn, 1), 0.0)
    elif first:
        extra_ref[...] = tab_ref[...]
    site = own_sum[3]
    if not first:
        total = total + before_ref[...]
        site = site + site_before_ref[...]
    spread_ref[...] = total
    for a in range(3):
        for block in blocks:
            line = a * 16 + (block // 2 + 1) * 4 + block % 2 + 1
            spread_ref[line : line + 1, :] += own_sum[a, block : block + 1, :]
    site_ref[...] = site
    if last:
        listed = list_ref[...]
        sent = jnp.zeros((16, 128), F32)
        for block in range(4):
            table = jnp.broadcast_to(site[block : block + 1], (16, 128))
            picked = jnp.take_along_axis(table, listed & 127, axis=1, mode="promise_in_bounds")
            sent = jnp.where(listed >> 7 == block, picked, sent)
        extra_ref[...] = sent


def force_call(tab, key, weights, blocks, layers, halo=None, before=None, listed=None):
    first, last = before is None, listed is not None
    count = len(blocks) * len(layers)
    args = [tab, key, *weights]
    if halo is not None:
        args.append(halo)
    if not first:
        args += before
    if last:
        args.append(listed)
    return pl.pallas_call(
        functools.partial(force_kernel, blocks, layers, first, last),
        out_shape=(
            jax.ShapeDtypeStruct((48, 128), F32),
            jax.ShapeDtypeStruct((8, 128), F32),
            jax.ShapeDtypeStruct((16 if last else 48, 128), F32),
        ),
        scratch_shapes=[
            pltpu.VMEM((9, count, ROWS, 128), F32),
            pltpu.VMEM((5, count, ROWS, 128), F32),
            pltpu.VMEM((128, 128), F32),
            pltpu.VMEM((4, 8, 128), F32),
            pltpu.VMEM((48, 128), F32),
        ]
        + [pltpu.VMEM((384, 768), BF16)] * count
        + [pltpu.VMEM((128, 768), F32)] * count,
        compiler_params=pltpu.CompilerParams(vmem_limit_bytes=40 * 1024 * 1024),
        cost_estimate=pl.CostEstimate(
            flops=count * 800_000_000, bytes_accessed=300_000, transcendentals=0
        ),
        name="force",
    )(*args)


def finish_kernel(
    arrived_ref, x_ref, below_ref, above_ref, pace_ref, place_ref, drift_ref, count_ref, *outs
):
    coords_ref, speed_ref, force_ref, rows_ref = outs
    lane = lax.broadcasted_iota(jnp.int32, (1, 128), 1)
    for row in range(4):
        line = arrived_ref[4 * row : 4 * row + 1, :]
        for part in range(1, 4):
            moved = pltpu.roll(arrived_ref[4 * row + part : 4 * row + part + 1, :], 32 * part, 1)
            line = jnp.where(lane // 32 == part, moved, line)
        rows_ref[row : row + 1, :] = line
    for cx in range(2):
        for cy in range(2):
            limit = jnp.zeros((1, 128), jnp.int32)
            for cz in range(4):
                limit = jnp.where(lane // 32 == cz, count_ref[cx, cy, cz], limit)
            occupied = lane % 32 < limit
            for a in range(3):
                beside = below_ref if cy == 0 else above_ref
                force = x_ref[a, cx, cy + 1 : cy + 2, :] + beside[a, cx]
                force_ref[a, cx, cy : cy + 1, :] = force
                speed = pace_ref[a, cx + 1, cy + 1 : cy + 2, :]
                speed_ref[a, cx, cy : cy + 1, :] = speed + 0.5 * TIME_STEP * force
                coords_ref[a, cx, cy : cy + 1, :] = jnp.where(
                    occupied,
                    place_ref[a, cx + 1, cy + 1 : cy + 2, :],
                    drift_ref[a, cx, cy : cy + 1, :] + TIME_STEP * speed,
                )


def prepare_weights(w_radial, w_env, w_latent, w_out):
    top = w_latent[0:128]
    both = jnp.dot(
        w_env.astype(F32), w_latent[128:256].astype(F32), precision=lax.Precision.HIGHEST
    )
    high = w_radial.astype(BF16)
    low = (w_radial - high.astype(F32)).astype(BF16)
    half = BF16(0.5)
    wr = jnp.concatenate([high, high, low, jnp.zeros_like(low)], axis=0).T * half
    wr = jnp.concatenate([jnp.pad(wr, ((0, 0), (0, 32))), jnp.pad(wr, ((0, 0), (32, 0)))], axis=0)
    wo = jnp.broadcast_to(w_out.astype(F32)[:, None], (128, 256))
    return (wr, top.T * half, top, (0.5 * both).T.astype(BF16), both.astype(BF16), wo)


def neighbour_keys(neighbours):
    code = neighbours.reshape(4, 6, 2, 2, 4, 32)
    offset = code // 32
    slot = code % 32
    grid = lambda n, dim: jnp.arange(n, dtype=jnp.int32).reshape(
        tuple(n if d == dim else 1 for d in range(6))
    )
    col = (grid(2, 2) + offset // 9) * 4 + grid(2, 3) + offset // 3 % 3
    place = (grid(4, 4) + offset % 3) * 32 + slot
    key = (col * 256 + place).transpose(2, 3, 4, 1, 0, 5).reshape(4, 4, USED, 128)
    return jnp.pad(key, ((0, 0), (0, 0), (0, ROWS - USED), (0, 0)))


def shifted(array, axis, step):
    peers = lax.axis_size(axis)
    return lax.ppermute(array, axis, [(i, (i + step) % peers) for i in range(peers)])


def both_ways(array, axis, dim, low, high):
    from_below = shifted(lax.slice_in_dim(array, *high, axis=dim), axis, 1)
    from_above = shifted(lax.slice_in_dim(array, *low, axis=dim), axis, -1)
    return from_below, from_above


def with_halo(array, axis, dim):
    below, above = both_ways(array, axis, dim, (0, 1), (1, 2))
    return jnp.concatenate([below, array, above], axis=dim)


def share(padded, axis, dim):
    below, above = both_ways(padded, axis, dim, (0, 2), (2, 4))
    return padded + jnp.concatenate([below, above], axis=dim)


def fold(padded, axis, dim):
    below, above = both_ways(padded, axis, dim, (0, 1), (3, 4))
    return lax.slice_in_dim(padded, 1, 3, axis=dim) + jnp.concatenate([below, above], axis=dim)


def on_device(
    positions,
    velocities,
    forces_in,
    counts,
    neighbours,
    send_list,
    w_radial,
    w_env,
    w_latent,
    w_out,
):
    weights = prepare_weights(w_radial, w_env, w_latent, w_out)
    key = neighbour_keys(neighbours)
    listed = jnp.pad(send_list.reshape(16, 32), ((0, 0), (0, 96)))
    occupied = jnp.arange(32, dtype=jnp.int32).reshape(1, 1, 1, 32) < counts[:, :, :, None]
    occupied = occupied.reshape(1, 2, 2, 128)
    half, quarter = TIME_STEP, 0.5 * TIME_STEP
    speed = velocities + quarter * forces_in
    coords = positions + half * speed

    def one_step(repeat, carry):
        wide_coords, wide_speed, change = carry
        change = lax.cond(
            repeat == 0, lambda part: part, lambda part: share(share(part, "gx", 1), "gy", 2), change
        )
        wide_coords = wide_coords + half * wide_speed + change[0:3]
        wide_speed = wide_speed + change[3:6]
        flat = wide_coords.reshape(48, 128)
        below = shifted(flat[:, 96:128], "gz", 1)
        *state, again = force_call(flat, key, weights, (0, 1), (1, 2))
        above = shifted(again[:, 0:32], "gz", -1)
        *state, rim = force_call(flat, key, weights, (0, 1, 2, 3), (0,), below, state)
        from_above = shifted(rim[:, 0:32], "gz", -1)
        *state, rim = force_call(flat, key, weights, (0, 1, 2, 3), (3,), above, state)
        from_below = shifted(rim[:, 96:128], "gz", 1)
        state = force_call(flat, key, weights, (2, 3), (1, 2), before=state, listed=listed)
        edges = jnp.concatenate([from_below, jnp.zeros((48, 64), F32), from_above], axis=1)
        force = (state[0] + edges).reshape(3, 4, 4, 128)
        change = jnp.concatenate([half * half * force, half * force], axis=0)
        return (wide_coords, wide_speed, change, force, state[2])

    first = jnp.concatenate([jnp.where(occupied, coords, UNOCCUPIED), speed], axis=0)
    first = with_halo(with_halo(first, "gx", 1), "gy", 2)
    zero = jnp.zeros((3, 4, 4, 128), F32)
    carry = (zero, zero, first, zero, jnp.zeros((16, 128), F32))
    wide_coords, wide_speed, _, force, sent = lax.fori_loop(
        0, STEPS, lambda repeat, carry: one_step(repeat, carry[0:3]), carry
    )
    work_energy = lax.all_to_all(sent, "gz", split_axis=0, concat_axis=0, tiled=True)
    force = fold(force, "gx", 1)
    below, above = both_ways(force, "gy", 2, (0, 1), (3, 4))
    own = jax.ShapeDtypeStruct((3, 2, 2, 128), F32)
    specs = [pl.BlockSpec(memory_space=pltpu.VMEM)] * 7 + [pl.BlockSpec(memory_space=pltpu.SMEM)]
    *moved, rows = pl.pallas_call(
        finish_kernel,
        out_shape=(own, own, own, jax.ShapeDtypeStruct((4, 128), F32)),
        in_specs=specs,
        name="finish",
    )(work_energy, force, below, above, wide_speed, wide_coords, coords, counts)
    return (*moved, rows.reshape(1, 1, 512))


def solution(mesh):
    split = P(None, "gx", "gy", "gz")
    cells = P("gx", "gy", "gz")
    return jax.shard_map(
        on_device,
        mesh=mesh,
        in_specs=(split, split, split, cells, split, cells, P(), P(), P(), P()),
        out_specs=(split, split, split, cells),
        check_vma=False,
    )
```

```python
import functools

import jax
import jax.numpy as jnp
from jax import lax
from jax.experimental import pallas as pl
from jax.experimental.pallas import tpu as pltpu
from jax.sharding import PartitionSpec as P

STEPS = 2
TIME_STEP = 0.5
BASIS = 8
CENTRE_FIRST = 0.5
CENTRE_STEP = 1.5 / 7.0
UNOCCUPIED = 1e30
FAR = 3.0
F32 = jnp.float32
BF16 = jnp.bfloat16

CELLS = 16
ROWS = 8
USED = 6
TILES = 3


def dot(a, b):
    return lax.dot_general(a, b, (((1,), (0,)), ((), ())), preferred_element_type=F32)


def dot_nt(a, b):
    return lax.dot_general(a, b, (((1,), (1,)), ((), ())), preferred_element_type=F32)


def pair_row(block, t):
    return jnp.concatenate([block[2 * t : 2 * t + 1], block[2 * t + 1 : 2 * t + 2]], axis=1)


def lane_pick(line, place, shape):
    table = jnp.broadcast_to(line, shape)
    return jnp.take_along_axis(table, place, axis=1, mode="promise_in_bounds")


def force_kernel(blocks, layers, first, last, *refs):
    refs = list(refs)
    outer = layers == (0, 3)
    tab_ref, key_ref = refs[:2]
    wr_ref, wtf_ref, wtop_ref, webf_ref, web_ref, wo_ref = refs[2:8]
    refs = refs[8:]
    if outer:
        below_ref, above_ref = refs.pop(0), refs.pop(0)
    if not first:
        before_ref, site_before_ref = refs[:2]
        refs = refs[2:]
    if last:
        list_ref = refs.pop(0)
    spread_ref, site_ref = refs[:2]
    refs = refs[2:]
    if outer:
        extra_ref = refs.pop(0)
    geo, res, acc, own_sum, table_ref = refs[:5]
    cells = [(block, layer) for block in blocks for layer in layers]
    count = len(cells)
    works, slopes = refs[5 : 5 + count], refs[5 + count :]
    lane48 = lax.broadcasted_iota(jnp.int32, (48, 128), 1)
    if outer:
        wide = jnp.zeros((48, 96), F32)
        below = jnp.concatenate([below_ref[...], wide], axis=1)
        above = pltpu.roll(jnp.concatenate([above_ref[...], wide], axis=1), 96, 1)
        table_ref[0] = jnp.where(lane48 < 32, below, pltpu.roll(tab_ref[...], 32, 1))
        table_ref[1] = jnp.where(lane48 < 96, pltpu.roll(tab_ref[...], 96, 1), above)
    else:
        table_ref[0] = tab_ref[...]
    bases = {0: 0, 1: 32, 2: 32, 3: 64}
    side = {0: 0, 1: 0, 2: 0, 3: 1}
    shape = (ROWS, 128)
    lane = lax.broadcasted_iota(jnp.int32, shape, 1)
    for k, (block, layer) in enumerate(cells):
        cx, cy = block // 2, block % 2
        base = bases[layer]
        own_place = 32 * (layer + 1) - base + lane % 32
        key = key_ref[block, layer]
        col = key >> 8
        place = (key & 255) - base
        own = []
        other = []
        for a in range(3):
            found = None
            for ox in range(3):
                for oy in range(3):
                    c = (cx + ox) * 4 + cy + oy
                    line = table_ref[side[layer], a * 16 + c : a * 16 + c + 1, :]
                    picked = lane_pick(line, place, shape)
                    found = picked if found is None else jnp.where(col == c, picked, found)
                    if ox == 1 and oy == 1:
                        own.append(lane_pick(line, own_place, shape))
            other.append(found)
        usable = jnp.logical_and(own[0] < 0.5 * UNOCCUPIED, other[0] < 0.5 * UNOCCUPIED)
        shift = (
            (col >> 2) - (cx + 1),
            (col & 3) - (cy + 1),
            (place + base) // 32 - (layer + 1),
        )
        far = (FAR, 0.0, 0.0)
        displace = [
            jnp.where(usable, other[a] - own[a] + shift[a].astype(F32), far[a]) for a in range(3)
        ]
        square = displace[0] ** 2 + displace[1] ** 2 + displace[2] ** 2
        radius = jnp.sqrt(square + 0.25)
        inverse = 1.0 / radius
        root = jnp.maximum(1.0 - 0.25 * square, 0.0)
        kept = [radius, root] + [displace[a] * inverse for a in range(3)] + displace
        kept.append(-4.0 * inverse * (root * root))
        for slot, value in enumerate(kept):
            geo[slot, k] = value

    same = lax.broadcasted_iota(jnp.int32, (32, 256), 1) % 32 == lax.broadcasted_iota(
        jnp.int32, (32, 256), 0
    )
    centre = CENTRE_FIRST + CENTRE_STEP * lax.broadcasted_iota(jnp.int32, (BASIS, 256), 0).astype(
        F32
    )

    def pair_of_cells(ks):
        lefts, mixeds, backs = {}, {}, {}
        for k in ks:
            work, slope = works[k], slopes[k]
            radius8 = geo[0, k]
            root8 = geo[1, k]
            scale8 = geo[8, k]
            dir8 = [geo[2 + a, k] for a in range(3)]
            for t in range(TILES):
                lanes = slice(256 * t, 256 * t + 256)
                away = pair_row(radius8, t) - centre
                radial = jnp.exp(-4.0 * away * away)
                steep = radial * (away * pair_row(scale8, t))
                high = radial.astype(BF16).astype(F32)
                steep_high = steep.astype(BF16).astype(F32)
                zero = jnp.zeros_like(high)
                stacked = jnp.concatenate(
                    [high, radial - high, high, zero, steep_high, steep - steep_high, steep_high, zero],
                    axis=0,
                ).astype(BF16)
                both = dot(wr_ref[...], stacked)
                zh = both[0:128]
                th = jnp.tanh(zh)
                up = 1.0 + th
                root = pair_row(root8, t)
                work[0:128, lanes] = (zh * up * (root * root)).astype(BF16)
                slope[:, lanes] = up * (
                    (1.0 + zh * (1.0 - th)) * both[128:256] - zh * (0.5 * root)
                )
                for a in range(3):
                    work[128 + 32 * a : 160 + 32 * a, lanes] = jnp.where(
                        same, pair_row(dir8[a], t), 0.0
                    ).astype(BF16)
                work[224:256, lanes] = jnp.zeros((32, 256), BF16)
        yield
        gathered = [dot_nt(works[k][0:128, :], works[k][128:256, :]).astype(BF16) for k in ks]
        mixed = dot(webf_ref[...], jnp.concatenate(gathered, axis=1))
        for i, k in enumerate(ks):
            part = mixed[:, 128 * i : 128 * i + 128]
            mixeds[k] = (2.0 * part.T).astype(BF16)
            lefts[k] = jnp.concatenate([wtf_ref[...], part.astype(BF16)], axis=1)
        yield
        for k in ks:
            work, left = works[k], lefts[k]
            root8 = geo[1, k]
            for t in range(TILES):
                lanes = slice(256 * t, 256 * t + 256)
                ph = dot(left, work[0:256, lanes])
                th = jnp.tanh(ph)
                up = 1.0 + th
                root = pair_row(root8, t)
                readout = wo_ref[...]
                energy = jnp.sum(readout * (ph * up), axis=0, keepdims=True)
                res[4, k, 2 * t : 2 * t + 1] = energy[:, 0:128]
                res[4, k, 2 * t + 1 : 2 * t + 2] = energy[:, 128:256]
                work[256:384, lanes] = (
                    (readout * (0.5 * root * root)) * (up * (1.0 + ph * (1.0 - th)))
                ).astype(BF16)
        yield
        gathered = [dot_nt(works[k][256:384, :], works[k][128:256, :]).astype(BF16) for k in ks]
        back = dot(web_ref[...], jnp.concatenate(gathered, axis=1))
        for i, k in enumerate(ks):
            part = back[:, 128 * i : 128 * i + 128]
            backs[k] = part.T.astype(BF16)
            lefts[k] = jnp.concatenate(
                [
                    jnp.concatenate([part.astype(BF16), wtop_ref[...]], axis=1),
                    jnp.concatenate([jnp.zeros((96, 128), BF16), mixeds[k][0:96]], axis=1),
                ],
                axis=0,
            )
        yield
        for k in ks:
            work, slope, left, back_t = works[k], slopes[k], lefts[k], backs[k]
            for t in range(TILES):
                lanes = slice(256 * t, 256 * t + 256)
                latent = work[0:128, lanes]
                slant = dot(left, work[128:384, lanes])
                turned = slant[128:224] + dot(back_t[0:96], latent)
                outcome = [
                    jnp.sum(jnp.where(same, turned[32 * a : 32 * a + 32], 0.0), axis=0, keepdims=True)
                    for a in range(3)
                ]
                outcome.append(jnp.sum(slant[0:128] * slope[:, lanes], axis=0, keepdims=True))
                for value, slot in zip(outcome, (0, 1, 2, 3)):
                    res[slot, k, 2 * t : 2 * t + 1] = value[:, 0:128]
                    res[slot, k, 2 * t + 1 : 2 * t + 2] = value[:, 128:256]

    runs = [pair_of_cells((k, k + 1)) for k in range(0, count, 2)]
    done = object()
    for tick in range(6 + len(runs)):
        for number in reversed(range(len(runs))):
            if tick >= number and runs[number] is not None:
                if next(runs[number], done) is done:
                    runs[number] = None

    radius, root = geo[0], geo[1]
    direction = [geo[2 + a] for a in range(3)]
    pull = [res[a] for a in range(3)]
    readout = res[4]
    inverse = 1.0 / radius
    along = pull[0] * direction[0] + pull[1] * direction[1] + pull[2] * direction[2]
    to_square = res[3] - 0.5 * (root * readout + inverse * inverse * along)
    for a in range(3):
        geo[2 + a] = pull[a] * inverse + geo[5 + a] * (2.0 * to_square)
    res[4] = root * root * readout

    acc[...] = jnp.zeros_like(acc)
    iota96 = lax.broadcasted_iota(jnp.int32, (96, 128), 0)
    iota16 = lax.broadcasted_iota(jnp.int32, (16, 128), 0)
    lane1 = lax.broadcasted_iota(jnp.int32, (1, 128), 1)
    own_sum[...] = jnp.zeros_like(own_sum)

    def spread_rows(col_row, terms):
        highs, lows = [], []
        for term in terms:
            chosen = jnp.where(col_row == iota16, term, 0.0)
            high = chosen.astype(BF16)
            highs.append(high)
            lows.append((chosen - high.astype(F32)).astype(BF16))
        return jnp.concatenate(highs + lows, axis=0)

    for k, (block, layer) in enumerate(cells):
        key = key_ref[block, layer]
        col = key >> 8
        place = (key & 255) - 32 * layer
        term = [geo[2 + a, k] for a in range(3)]
        hots, lefts = [], []
        for r in range(USED):
            hots.append(jnp.where(iota96 == place[r : r + 1], 1.0, 0.0).astype(BF16))
            lefts.append(spread_rows(col[r : r + 1], [-term[a][r : r + 1] for a in range(3)]))
        added = dot_nt(jnp.concatenate(hots, axis=1), jnp.concatenate(lefts, axis=1))
        at = 32 * layer - bases[layer]
        acc[side[layer], at : at + 96, 0:96] += added
        term.append(res[4, k])
        for slot in range(4):
            line = jnp.sum(term[slot][0:USED], axis=0, keepdims=True)
            line = line + pltpu.roll(line, 32, 1)
            line = line + pltpu.roll(line, 64, 1)
            own_sum[slot, block : block + 1, :] += jnp.where(lane1 // 32 == layer, line, 0.0)

    flipped = acc[0].T
    total = flipped[0:48] + flipped[48:96]
    if outer:
        flipped = acc[1].T
        upper = flipped[0:48] + flipped[48:96]
        extra_ref[...] = jnp.where(lane48 < 96, total, upper)
        total = jnp.where(lane48 < 96, pltpu.roll(total, 96, 1), 0.0) + jnp.where(
            lane48 >= 32, pltpu.roll(upper, 32, 1), 0.0
        )
    site = own_sum[3]
    if not first:
        total = total + before_ref[...]
        site = site + site_before_ref[...]
    spread_ref[...] = total
    for a in range(3):
        for block in blocks:
            line = a * 16 + (block // 2 + 1) * 4 + block % 2 + 1
            spread_ref[line : line + 1, :] += own_sum[a, block : block + 1, :]
    if not last:
        site_ref[...] = site
    else:
        listed = list_ref[...]
        sent = jnp.zeros((16, 128), F32)
        for block in range(4):
            table = jnp.broadcast_to(site[block : block + 1], (16, 128))
            picked = jnp.take_along_axis(table, listed & 127, axis=1, mode="promise_in_bounds")
            sent = jnp.where(listed >> 7 == block, picked, sent)
        site_ref[...] = sent


def force_call(tab, key, weights, blocks, layers, halo=(), before=None, listed=None):
    first, last = before is None, listed is not None
    count = len(blocks) * len(layers)
    args = [tab, key, *weights, *halo]
    if not first:
        args += before
    if last:
        args.append(listed)
    outs = [48, 16 if last else 8] + [48] * len(halo[:1])
    return pl.pallas_call(
        functools.partial(force_kernel, blocks, layers, first, last),
        out_shape=tuple(jax.ShapeDtypeStruct((rows, 128), F32) for rows in outs),
        scratch_shapes=[
            pltpu.VMEM((9, count, ROWS, 128), F32),
            pltpu.VMEM((5, count, ROWS, 128), F32),
            pltpu.VMEM((2, 128, 128), F32),
            pltpu.VMEM((4, 8, 128), F32),
            pltpu.VMEM((2, 48, 128), F32),
        ]
        + [pltpu.VMEM((384, 768), BF16)] * count
        + [pltpu.VMEM((128, 768), F32)] * count,
        compiler_params=pltpu.CompilerParams(vmem_limit_bytes=40 * 1024 * 1024),
        cost_estimate=pl.CostEstimate(
            flops=count * 800_000_000, bytes_accessed=300_000, transcendentals=0
        ),
        name="force",
    )(*args)


def finish_kernel(
    arrived_ref, x_ref, below_ref, above_ref, pace_ref, place_ref, drift_ref, count_ref, *outs
):
    coords_ref, speed_ref, force_ref, rows_ref = outs
    lane = lax.broadcasted_iota(jnp.int32, (1, 128), 1)
    for row in range(4):
        line = arrived_ref[4 * row : 4 * row + 1, :]
        for part in range(1, 4):
            moved = pltpu.roll(arrived_ref[4 * row + part : 4 * row + part + 1, :], 32 * part, 1)
            line = jnp.where(lane // 32 == part, moved, line)
        rows_ref[row : row + 1, :] = line
    for cx in range(2):
        for cy in range(2):
            limit = jnp.zeros((1, 128), jnp.int32)
            for cz in range(4):
                limit = jnp.where(lane // 32 == cz, count_ref[cx, cy, cz], limit)
            occupied = lane % 32 < limit
            for a in range(3):
                beside = below_ref if cy == 0 else above_ref
                force = x_ref[a, cx, cy + 1 : cy + 2, :] + beside[a, cx]
                force_ref[a, cx, cy : cy + 1, :] = force
                speed = pace_ref[a, cx + 1, cy + 1 : cy + 2, :]
                speed_ref[a, cx, cy : cy + 1, :] = speed + 0.5 * TIME_STEP * force
                coords_ref[a, cx, cy : cy + 1, :] = jnp.where(
                    occupied,
                    place_ref[a, cx + 1, cy + 1 : cy + 2, :],
                    drift_ref[a, cx, cy : cy + 1, :] + TIME_STEP * speed,
                )


def prepare_weights(w_radial, w_env, w_latent, w_out):
    top = w_latent[0:128]
    both = jnp.dot(
        w_env.astype(F32), w_latent[128:256].astype(F32), precision=lax.Precision.HIGHEST
    )
    high = w_radial.astype(BF16)
    low = (w_radial - high.astype(F32)).astype(BF16)
    half = BF16(0.5)
    wr = jnp.concatenate([high, high, low, jnp.zeros_like(low)], axis=0).T * half
    wr = jnp.concatenate([jnp.pad(wr, ((0, 0), (0, 32))), jnp.pad(wr, ((0, 0), (32, 0)))], axis=0)
    wo = jnp.broadcast_to(w_out.astype(F32)[:, None], (128, 256))
    return (wr, top.T * half, top, (0.5 * both).T.astype(BF16), both.astype(BF16), wo)


def neighbour_keys(neighbours):
    code = neighbours.reshape(4, 6, 2, 2, 4, 32)
    offset = code // 32
    slot = code % 32
    grid = lambda n, dim: jnp.arange(n, dtype=jnp.int32).reshape(
        tuple(n if d == dim else 1 for d in range(6))
    )
    col = (grid(2, 2) + offset // 9) * 4 + grid(2, 3) + offset // 3 % 3
    place = (grid(4, 4) + offset % 3) * 32 + slot
    key = (col * 256 + place).transpose(2, 3, 4, 1, 0, 5).reshape(4, 4, USED, 128)
    return jnp.pad(key, ((0, 0), (0, 0), (0, ROWS - USED), (0, 0)))


def shifted(array, axis, step):
    peers = lax.axis_size(axis)
    return lax.ppermute(array, axis, [(i, (i + step) % peers) for i in range(peers)])


def both_ways(array, axis, dim, low, high):
    from_below = shifted(lax.slice_in_dim(array, *high, axis=dim), axis, 1)
    from_above = shifted(lax.slice_in_dim(array, *low, axis=dim), axis, -1)
    return from_below, from_above


def with_halo(array, axis, dim):
    below, above = both_ways(array, axis, dim, (0, 1), (1, 2))
    return jnp.concatenate([below, array, above], axis=dim)


def share(padded, axis, dim):
    below, above = both_ways(padded, axis, dim, (0, 2), (2, 4))
    return padded + jnp.concatenate([below, above], axis=dim)


def fold(padded, axis, dim):
    below, above = both_ways(padded, axis, dim, (0, 1), (3, 4))
    return lax.slice_in_dim(padded, 1, 3, axis=dim) + jnp.concatenate([below, above], axis=dim)


def on_device(
    positions,
    velocities,
    forces_in,
    counts,
    neighbours,
    send_list,
    w_radial,
    w_env,
    w_latent,
    w_out,
):
    weights = prepare_weights(w_radial, w_env, w_latent, w_out)
    key = neighbour_keys(neighbours)
    listed = jnp.pad(send_list.reshape(16, 32), ((0, 0), (0, 96)))
    occupied = jnp.arange(32, dtype=jnp.int32).reshape(1, 1, 1, 32) < counts[:, :, :, None]
    occupied = occupied.reshape(1, 2, 2, 128)
    half, quarter = TIME_STEP, 0.5 * TIME_STEP
    speed = velocities + quarter * forces_in
    coords = positions + half * speed

    def one_step(repeat, carry):
        wide_coords, wide_speed, change = carry
        change = lax.cond(
            repeat == 0, lambda part: part, lambda part: share(share(part, "gx", 1), "gy", 2), change
        )
        wide_coords = wide_coords + half * wide_speed + change[0:3]
        wide_speed = wide_speed + change[3:6]
        flat = wide_coords.reshape(48, 128)
        halo = shifted(flat[:, 96:128], "gz", 1), shifted(flat[:, 0:32], "gz", -1)
        state = force_call(flat, key, weights, (0, 1), (1, 2))
        *state, rim = force_call(flat, key, weights, (0, 1, 2, 3), (0, 3), halo, state)
        from_below = shifted(rim[:, 96:128], "gz", 1)
        from_above = shifted(rim[:, 0:32], "gz", -1)
        spread, sent = force_call(
            flat, key, weights, (2, 3), (1, 2), before=state, listed=listed
        )
        edges = jnp.concatenate([from_below, jnp.zeros((48, 64), F32), from_above], axis=1)
        force = (spread + edges).reshape(3, 4, 4, 128)
        change = jnp.concatenate([half * half * force, half * force], axis=0)
        return (wide_coords, wide_speed, change, force, sent)

    first = jnp.concatenate([jnp.where(occupied, coords, UNOCCUPIED), speed], axis=0)
    first = with_halo(with_halo(first, "gx", 1), "gy", 2)
    zero = jnp.zeros((3, 4, 4, 128), F32)
    carry = (zero, zero, first, zero, jnp.zeros((16, 128), F32))
    wide_coords, wide_speed, _, force, sent = lax.fori_loop(
        0, STEPS, lambda repeat, carry: one_step(repeat, carry[0:3]), carry
    )
    work_energy = lax.all_to_all(sent, "gz", split_axis=0, concat_axis=0, tiled=True)
    force = fold(force, "gx", 1)
    below, above = both_ways(force, "gy", 2, (0, 1), (3, 4))
    own = jax.ShapeDtypeStruct((3, 2, 2, 128), F32)
    specs = [pl.BlockSpec(memory_space=pltpu.VMEM)] * 7 + [pl.BlockSpec(memory_space=pltpu.SMEM)]
    *moved, rows = pl.pallas_call(
        finish_kernel,
        out_shape=(own, own, own, jax.ShapeDtypeStruct((4, 128), F32)),
        in_specs=specs,
        name="finish",
    )(work_energy, force, below, above, wide_speed, wide_coords, coords, counts)
    return (*moved, rows.reshape(1, 1, 512))


def solution(mesh):
    split = P(None, "gx", "gy", "gz")
    cells = P("gx", "gy", "gz")
    return jax.shard_map(
        on_device,
        mesh=mesh,
        in_specs=(split, split, split, cells, split, cells, P(), P(), P(), P()),
        out_specs=(split, split, split, cells),
        check_vma=False,
    )
```

```python
import functools

import jax
import jax.numpy as jnp
from jax import lax
from jax.experimental import pallas as pl
from jax.experimental.pallas import tpu as pltpu
from jax.sharding import PartitionSpec as P

STEPS = 2
TIME_STEP = 0.5
BASIS = 8
CENTRE_FIRST = 0.5
CENTRE_STEP = 1.5 / 7.0
UNOCCUPIED = 1e30
FAR = 3.0
F32 = jnp.float32
BF16 = jnp.bfloat16

CELLS = 16
ROWS = 8
USED = 6
TILES = 3


def dot(a, b):
    return lax.dot_general(a, b, (((1,), (0,)), ((), ())), preferred_element_type=F32)


def dot_nt(a, b):
    return lax.dot_general(a, b, (((1,), (1,)), ((), ())), preferred_element_type=F32)


def pair_row(block, t):
    return jnp.concatenate([block[2 * t : 2 * t + 1], block[2 * t + 1 : 2 * t + 2]], axis=1)


def lane_pick(line, place, shape):
    table = jnp.broadcast_to(line, shape)
    return jnp.take_along_axis(table, place, axis=1, mode="promise_in_bounds")


def force_kernel(blocks, layers, first, last, *refs):
    refs = list(refs)
    outer = layers == (0, 3)
    tab_ref, key_ref = refs[:2]
    wr_ref, wtf_ref, wtop_ref, webf_ref, web_ref, wo_ref = refs[2:8]
    refs = refs[8:]
    if outer:
        below_ref, above_ref = refs.pop(0), refs.pop(0)
    if not first:
        before_ref, site_before_ref = refs[:2]
        refs = refs[2:]
    if last:
        list_ref = refs.pop(0)
    spread_ref, site_ref = refs[:2]
    refs = refs[2:]
    if outer:
        extra_ref = refs.pop(0)
    geo, res, acc, own_sum, table_ref = refs[:5]
    cells = [(block, layer) for block in blocks for layer in layers]
    count = len(cells)
    works, slopes = refs[5 : 5 + count], refs[5 + count :]
    lane48 = lax.broadcasted_iota(jnp.int32, (48, 128), 1)
    if outer:
        wide = jnp.zeros((48, 96), F32)
        below = jnp.concatenate([below_ref[...], wide], axis=1)
        above = pltpu.roll(jnp.concatenate([above_ref[...], wide], axis=1), 96, 1)
        table_ref[0] = jnp.where(lane48 < 32, below, pltpu.roll(tab_ref[...], 32, 1))
        table_ref[1] = jnp.where(lane48 < 96, pltpu.roll(tab_ref[...], 96, 1), above)
    else:
        table_ref[0] = tab_ref[...]
    bases = {0: 0, 1: 32, 2: 32, 3: 64}
    side = {0: 0, 1: 0, 2: 0, 3: 1}
    shape = (ROWS, 128)
    lane = lax.broadcasted_iota(jnp.int32, shape, 1)
    for k, (block, layer) in enumerate(cells):
        cx, cy = block // 2, block % 2
        base = bases[layer]
        own_place = 32 * (layer + 1) - base + lane % 32
        key = key_ref[block, layer]
        col = key >> 8
        place = (key & 255) - base
        own = []
        other = []
        for a in range(3):
            found = None
            for ox in range(3):
                for oy in range(3):
                    c = (cx + ox) * 4 + cy + oy
                    line = table_ref[side[layer], a * 16 + c : a * 16 + c + 1, :]
                    picked = lane_pick(line, place, shape)
                    found = picked if found is None else jnp.where(col == c, picked, found)
                    if ox == 1 and oy == 1:
                        own.append(lane_pick(line, own_place, shape))
            other.append(found)
        usable = jnp.logical_and(own[0] < 0.5 * UNOCCUPIED, other[0] < 0.5 * UNOCCUPIED)
        shift = (
            (col >> 2) - (cx + 1),
            (col & 3) - (cy + 1),
            (place + base) // 32 - (layer + 1),
        )
        far = (FAR, 0.0, 0.0)
        displace = [
            jnp.where(usable, other[a] - own[a] + shift[a].astype(F32), far[a]) for a in range(3)
        ]
        square = displace[0] ** 2 + displace[1] ** 2 + displace[2] ** 2
        radius = jnp.sqrt(square + 0.25)
        inverse = 1.0 / radius
        root = jnp.maximum(1.0 - 0.25 * square, 0.0)
        kept = [radius, root] + [displace[a] * inverse for a in range(3)] + displace
        kept.append(-4.0 * inverse * (root * root))
        for slot, value in enumerate(kept):
            geo[slot, k] = value

    same = lax.broadcasted_iota(jnp.int32, (32, 256), 1) % 32 == lax.broadcasted_iota(
        jnp.int32, (32, 256), 0
    )
    centre = CENTRE_FIRST + CENTRE_STEP * lax.broadcasted_iota(jnp.int32, (BASIS, 256), 0).astype(
        F32
    )

    def pair_of_cells(ks):
        lefts, mixeds, backs = {}, {}, {}
        for k in ks:
            work, slope = works[k], slopes[k]
            radius8 = geo[0, k]
            root8 = geo[1, k]
            scale8 = geo[8, k]
            dir8 = [geo[2 + a, k] for a in range(3)]
            for t in range(TILES):
                lanes = slice(256 * t, 256 * t + 256)
                away = pair_row(radius8, t) - centre
                radial = jnp.exp(-4.0 * away * away)
                steep = radial * (away * pair_row(scale8, t))
                high = radial.astype(BF16).astype(F32)
                steep_high = steep.astype(BF16).astype(F32)
                zero = jnp.zeros_like(high)
                stacked = jnp.concatenate(
                    [high, radial - high, high, zero, steep_high, steep - steep_high, steep_high, zero],
                    axis=0,
                ).astype(BF16)
                both = dot(wr_ref[...], stacked)
                zh = both[0:128]
                th = jnp.tanh(zh)
                up = 1.0 + th
                root = pair_row(root8, t)
                work[0:128, lanes] = (zh * up * (root * root)).astype(BF16)
                slope[:, lanes] = up * (
                    (1.0 + zh * (1.0 - th)) * both[128:256] - zh * (0.5 * root)
                )
                for a in range(3):
                    work[128 + 32 * a : 160 + 32 * a, lanes] = jnp.where(
                        same, pair_row(dir8[a], t), 0.0
                    ).astype(BF16)
                work[224:256, lanes] = jnp.zeros((32, 256), BF16)
        yield
        gathered = [dot_nt(works[k][0:128, :], works[k][128:256, :]).astype(BF16) for k in ks]
        mixed = dot(webf_ref[...], jnp.concatenate(gathered, axis=1))
        for i, k in enumerate(ks):
            part = mixed[:, 128 * i : 128 * i + 128]
            mixeds[k] = (2.0 * part.T).astype(BF16)
            lefts[k] = jnp.concatenate([wtf_ref[...], part.astype(BF16)], axis=1)
        yield
        for k in ks:
            work, left = works[k], lefts[k]
            root8 = geo[1, k]
            for t in range(TILES):
                lanes = slice(256 * t, 256 * t + 256)
                ph = dot(left, work[0:256, lanes])
                th = jnp.tanh(ph)
                up = 1.0 + th
                root = pair_row(root8, t)
                readout = wo_ref[...]
                energy = jnp.sum(readout * (ph * up), axis=0, keepdims=True)
                res[4, k, 2 * t : 2 * t + 1] = energy[:, 0:128]
                res[4, k, 2 * t + 1 : 2 * t + 2] = energy[:, 128:256]
                work[256:384, lanes] = (
                    (readout * (0.5 * root * root)) * (up * (1.0 + ph * (1.0 - th)))
                ).astype(BF16)
        yield
        gathered = [dot_nt(works[k][256:384, :], works[k][128:256, :]).astype(BF16) for k in ks]
        back = dot(web_ref[...], jnp.concatenate(gathered, axis=1))
        for i, k in enumerate(ks):
            part = back[:, 128 * i : 128 * i + 128]
            backs[k] = part.T.astype(BF16)
            lefts[k] = jnp.concatenate(
                [
                    jnp.concatenate([part.astype(BF16), wtop_ref[...]], axis=1),
                    jnp.concatenate([jnp.zeros((96, 128), BF16), mixeds[k][0:96]], axis=1),
                ],
                axis=0,
            )
        yield
        for k in ks:
            work, slope, left, back_t = works[k], slopes[k], lefts[k], backs[k]
            for t in range(TILES):
                lanes = slice(256 * t, 256 * t + 256)
                latent = work[0:128, lanes]
                slant = dot(left, work[128:384, lanes])
                turned = slant[128:224] + dot(back_t[0:96], latent)
                outcome = [
                    jnp.sum(jnp.where(same, turned[32 * a : 32 * a + 32], 0.0), axis=0, keepdims=True)
                    for a in range(3)
                ]
                outcome.append(jnp.sum(slant[0:128] * slope[:, lanes], axis=0, keepdims=True))
                for value, slot in zip(outcome, (0, 1, 2, 3)):
                    res[slot, k, 2 * t : 2 * t + 1] = value[:, 0:128]
                    res[slot, k, 2 * t + 1 : 2 * t + 2] = value[:, 128:256]

    runs = [pair_of_cells((k, k + 1)) for k in range(0, count, 2)]
    done = object()
    for tick in range(6 + len(runs)):
        for number in reversed(range(len(runs))):
            if tick >= number and runs[number] is not None:
                if next(runs[number], done) is done:
                    runs[number] = None

    radius, root = geo[0], geo[1]
    direction = [geo[2 + a] for a in range(3)]
    pull = [res[a] for a in range(3)]
    readout = res[4]
    inverse = 1.0 / radius
    along = pull[0] * direction[0] + pull[1] * direction[1] + pull[2] * direction[2]
    to_square = res[3] - 0.5 * (root * readout + inverse * inverse * along)
    for a in range(3):
        geo[2 + a] = pull[a] * inverse + geo[5 + a] * (2.0 * to_square)
    res[4] = root * root * readout

    acc[...] = jnp.zeros_like(acc)
    iota96 = lax.broadcasted_iota(jnp.int32, (96, 128), 0)
    iota16 = lax.broadcasted_iota(jnp.int32, (16, 128), 0)
    lane1 = lax.broadcasted_iota(jnp.int32, (1, 128), 1)
    own_sum[...] = jnp.zeros_like(own_sum)

    def spread_rows(col_row, terms):
        highs, lows = [], []
        for term in terms:
            chosen = jnp.where(col_row == iota16, term, 0.0)
            high = chosen.astype(BF16)
            highs.append(high)
            lows.append((chosen - high.astype(F32)).astype(BF16))
        return jnp.concatenate(highs + lows, axis=0)

    for k, (block, layer) in enumerate(cells):
        key = key_ref[block, layer]
        col = key >> 8
        place = (key & 255) - 32 * layer
        term = [geo[2 + a, k] for a in range(3)]
        hots, lefts = [], []
        for r in range(USED):
            hots.append(jnp.where(iota96 == place[r : r + 1], 1.0, 0.0).astype(BF16))
            lefts.append(spread_rows(col[r : r + 1], [-term[a][r : r + 1] for a in range(3)]))
        added = dot_nt(jnp.concatenate(hots, axis=1), jnp.concatenate(lefts, axis=1))
        at = 32 * layer - bases[layer]
        acc[side[layer], at : at + 96, 0:96] += added
        term.append(res[4, k])
        for slot in range(4):
            line = jnp.sum(term[slot][0:USED], axis=0, keepdims=True)
            line = line + pltpu.roll(line, 32, 1)
            line = line + pltpu.roll(line, 64, 1)
            own_sum[slot, block : block + 1, :] += jnp.where(lane1 // 32 == layer, line, 0.0)

    flipped = acc[0].T
    total = flipped[0:48] + flipped[48:96]
    if outer:
        flipped = acc[1].T
        upper = flipped[0:48] + flipped[48:96]
        extra_ref[...] = jnp.where(lane48 < 96, total, upper)
        total = jnp.where(lane48 < 96, pltpu.roll(total, 96, 1), 0.0) + jnp.where(
            lane48 >= 32, pltpu.roll(upper, 32, 1), 0.0
        )
    site = own_sum[3]
    if not first:
        total = total + before_ref[...]
        site = site + site_before_ref[...]
    spread_ref[...] = total
    for a in range(3):
        for block in blocks:
            line = a * 16 + (block // 2 + 1) * 4 + block % 2 + 1
            spread_ref[line : line + 1, :] += own_sum[a, block : block + 1, :]
    if not last:
        site_ref[...] = site
    else:
        listed = list_ref[...]
        sent = jnp.zeros((16, 128), F32)
        for block in range(4):
            table = jnp.broadcast_to(site[block : block + 1], (16, 128))
            picked = jnp.take_along_axis(table, listed & 127, axis=1, mode="promise_in_bounds")
            sent = jnp.where(listed >> 7 == block, picked, sent)
        site_ref[...] = sent


def force_call(tab, key, weights, blocks, layers, halo=(), before=None, listed=None):
    first, last = before is None, listed is not None
    count = len(blocks) * len(layers)
    args = [tab, key, *weights, *halo]
    if not first:
        args += before
    if last:
        args.append(listed)
    outs = [48, 16 if last else 8] + [48] * len(halo[:1])
    return pl.pallas_call(
        functools.partial(force_kernel, blocks, layers, first, last),
        out_shape=tuple(jax.ShapeDtypeStruct((rows, 128), F32) for rows in outs),
        scratch_shapes=[
            pltpu.VMEM((9, count, ROWS, 128), F32),
            pltpu.VMEM((5, count, ROWS, 128), F32),
            pltpu.VMEM((2, 128, 128), F32),
            pltpu.VMEM((4, 8, 128), F32),
            pltpu.VMEM((2, 48, 128), F32),
        ]
        + [pltpu.VMEM((384, 768), BF16)] * count
        + [pltpu.VMEM((128, 768), F32)] * count,
        compiler_params=pltpu.CompilerParams(vmem_limit_bytes=40 * 1024 * 1024),
        cost_estimate=pl.CostEstimate(
            flops=count * 800_000_000, bytes_accessed=300_000, transcendentals=0
        ),
        name="force",
    )(*args)


def lanes_below(count_ref, cx, cy):
    lane = lax.broadcasted_iota(jnp.int32, (1, 128), 1)
    limit = jnp.zeros((1, 128), jnp.int32)
    for cz in range(4):
        limit = jnp.where(lane // 32 == cz, count_ref[cx, cy, cz], limit)
    return lane % 32 < limit


def begin_kernel(
    positions_ref, velocities_ref, forces_ref, count_ref, low_ref, high_ref, coords_ref
):
    speed = velocities_ref[...] + 0.5 * TIME_STEP * forces_ref[...]
    coords = positions_ref[...] + TIME_STEP * speed
    coords_ref[...] = coords + TIME_STEP * speed
    for cx, first_ref in enumerate((low_ref, high_ref)):
        first_ref[3:6, 0] = speed[:, cx]
        for cy in range(2):
            occupied = lanes_below(count_ref, cx, cy)
            for a in range(3):
                first_ref[a, 0, cy : cy + 1, :] = jnp.where(
                    occupied, coords[a, cx, cy : cy + 1, :], UNOCCUPIED
                )


def finish_kernel(
    source_ref, x_ref, below_ref, above_ref, pace_ref, place_ref, drift_ref, count_ref, *outs
):
    coords_ref, speed_ref, force_ref, rows_ref, arrived_ref, semaphore = outs
    copy = pltpu.make_async_copy(source_ref, arrived_ref, semaphore)
    copy.start()
    for cx in range(2):
        for cy in range(2):
            occupied = lanes_below(count_ref, cx, cy)
            for a in range(3):
                beside = below_ref if cy == 0 else above_ref
                force = x_ref[a, cx, cy + 1 : cy + 2, :] + beside[a, cx]
                force_ref[a, cx, cy : cy + 1, :] = force
                speed = pace_ref[a, cx + 1, cy + 1 : cy + 2, :]
                speed_ref[a, cx, cy : cy + 1, :] = speed + 0.5 * TIME_STEP * force
                coords_ref[a, cx, cy : cy + 1, :] = jnp.where(
                    occupied,
                    place_ref[a, cx + 1, cy + 1 : cy + 2, :],
                    drift_ref[a, cx, cy : cy + 1, :],
                )
    copy.wait()
    lane = lax.broadcasted_iota(jnp.int32, (1, 128), 1)
    for row in range(4):
        line = arrived_ref[4 * row : 4 * row + 1, :]
        for part in range(1, 4):
            moved = pltpu.roll(arrived_ref[4 * row + part : 4 * row + part + 1, :], 32 * part, 1)
            line = jnp.where(lane // 32 == part, moved, line)
        rows_ref[row : row + 1, :] = line


def prepare_weights(w_radial, w_env, w_latent, w_out):
    top = w_latent[0:128]
    both = jnp.dot(
        w_env.astype(F32), w_latent[128:256].astype(F32), precision=lax.Precision.HIGHEST
    )
    high = w_radial.astype(BF16)
    low = (w_radial - high.astype(F32)).astype(BF16)
    half = BF16(0.5)
    wr = jnp.concatenate([high, high, low, jnp.zeros_like(low)], axis=0).T * half
    wr = jnp.concatenate([jnp.pad(wr, ((0, 0), (0, 32))), jnp.pad(wr, ((0, 0), (32, 0)))], axis=0)
    wo = jnp.broadcast_to(w_out.astype(F32)[:, None], (128, 256))
    return (wr, top.T * half, top, (0.5 * both).T.astype(BF16), both.astype(BF16), wo)


def neighbour_keys(neighbours):
    code = neighbours.reshape(4, 6, 2, 2, 4, 32)
    offset = code // 32
    slot = code % 32
    grid = lambda n, dim: jnp.arange(n, dtype=jnp.int32).reshape(
        tuple(n if d == dim else 1 for d in range(6))
    )
    col = (grid(2, 2) + offset // 9) * 4 + grid(2, 3) + offset // 3 % 3
    place = (grid(4, 4) + offset % 3) * 32 + slot
    key = (col * 256 + place).transpose(2, 3, 4, 1, 0, 5).reshape(4, 4, USED, 128)
    return jnp.pad(key, ((0, 0), (0, 0), (0, ROWS - USED), (0, 0)))


def shifted(array, axis, step):
    peers = lax.axis_size(axis)
    return lax.ppermute(array, axis, [(i, (i + step) % peers) for i in range(peers)])


def both_ways(array, axis, dim, low, high):
    from_below = shifted(lax.slice_in_dim(array, *high, axis=dim), axis, 1)
    from_above = shifted(lax.slice_in_dim(array, *low, axis=dim), axis, -1)
    return from_below, from_above


def with_halo(array, axis, dim):
    below, above = both_ways(array, axis, dim, (0, 1), (1, 2))
    return jnp.concatenate([below, array, above], axis=dim)


def share(padded, axis, dim):
    below, above = both_ways(padded, axis, dim, (0, 2), (2, 4))
    return padded + jnp.concatenate([below, above], axis=dim)


def on_device(
    positions,
    velocities,
    forces_in,
    counts,
    neighbours,
    send_list,
    w_radial,
    w_env,
    w_latent,
    w_out,
):
    weights = prepare_weights(w_radial, w_env, w_latent, w_out)
    key = neighbour_keys(neighbours)
    listed = jnp.pad(send_list.reshape(16, 32), ((0, 0), (0, 96)))
    half = TIME_STEP
    own = jax.ShapeDtypeStruct((3, 2, 2, 128), F32)
    vmem, smem = (pl.BlockSpec(memory_space=space) for space in (pltpu.VMEM, pltpu.SMEM))
    face = jax.ShapeDtypeStruct((6, 1, 2, 128), F32)
    low, high, drift = pl.pallas_call(
        begin_kernel,
        out_shape=(face, face, own),
        in_specs=[vmem] * 3 + [smem],
        name="begin",
    )(positions, velocities, forces_in, counts)
    first = jnp.concatenate([shifted(high, "gx", 1), low, high, shifted(low, "gx", -1)], axis=1)
    first = with_halo(first, "gy", 2)

    def one_step(repeat, carry):
        wide_coords, wide_speed, force = carry[0:3]

        def from_force(part):
            part = share(share(part, "gx", 1), "gy", 2)
            return jnp.concatenate([half * half * part, half * part], axis=0)

        change = lax.cond(repeat == 0, lambda part: first, from_force, force)
        wide_coords = wide_coords + half * wide_speed + change[0:3]
        wide_speed = wide_speed + change[3:6]
        flat = wide_coords.reshape(48, 128)
        halo = shifted(flat[:, 96:128], "gz", 1), shifted(flat[:, 0:32], "gz", -1)
        state = force_call(flat, key, weights, (0, 1), (1, 2))
        *state, rim = force_call(flat, key, weights, (0, 1, 2, 3), (0, 3), halo, state)
        from_below = shifted(rim[:, 96:128], "gz", 1)
        from_above = shifted(rim[:, 0:32], "gz", -1)
        spread, sent = force_call(
            flat, key, weights, (2, 3), (1, 2), before=state, listed=listed
        )
        edges = jnp.concatenate([from_below, jnp.zeros((48, 64), F32), from_above], axis=1)
        force = (spread + edges).reshape(3, 4, 4, 128)
        return (wide_coords, wide_speed, force, force[:, 0:1], force[:, 3:4], sent)

    zero = jnp.zeros((3, 4, 4, 128), F32)
    carry = (zero, zero, zero, zero[:, 0:1], zero[:, 0:1], jnp.zeros((16, 128), F32))
    wide_coords, wide_speed, force, low, high, sent = lax.fori_loop(0, STEPS, one_step, carry)
    work_energy = lax.all_to_all(sent, "gz", split_axis=0, concat_axis=0, tiled=True)
    force = force[:, 1:3] + jnp.concatenate(
        [shifted(high, "gx", 1), shifted(low, "gx", -1)], axis=1
    )
    below, above = both_ways(force, "gy", 2, (0, 1), (3, 4))
    *moved, rows = pl.pallas_call(
        finish_kernel,
        out_shape=(own, own, own, jax.ShapeDtypeStruct((4, 128), F32)),
        in_specs=[pl.BlockSpec(memory_space=pltpu.HBM)] + [vmem] * 6 + [smem],
        scratch_shapes=[pltpu.VMEM((16, 128), F32), pltpu.SemaphoreType.DMA(())],
        name="finish",
    )(work_energy, force, below, above, wide_speed, wide_coords, drift, counts)
    return (*moved, rows.reshape(1, 1, 512))


def solution(mesh):
    split = P(None, "gx", "gy", "gz")
    cells = P("gx", "gy", "gz")
    return jax.shard_map(
        on_device,
        mesh=mesh,
        in_specs=(split, split, split, cells, split, cells, P(), P(), P(), P()),
        out_specs=(split, split, split, cells),
        check_vma=False,
    )
```

```python
import functools

import jax
import jax.numpy as jnp
from jax import lax
from jax.experimental import pallas as pl
from jax.experimental.pallas import tpu as pltpu
from jax.sharding import PartitionSpec as P

STEPS = 2
TIME_STEP = 0.5
BASIS = 8
CENTRE_FIRST = 0.5
CENTRE_STEP = 1.5 / 7.0
UNOCCUPIED = 1e30
FAR = 3.0
F32 = jnp.float32
BF16 = jnp.bfloat16

CELLS = 16
ROWS = 8
USED = 6
TILES = 3


def dot(a, b):
    return lax.dot_general(a, b, (((1,), (0,)), ((), ())), preferred_element_type=F32)


def dot_nt(a, b):
    return lax.dot_general(a, b, (((1,), (1,)), ((), ())), preferred_element_type=F32)


def pair_row(block, t):
    return jnp.concatenate([block[2 * t : 2 * t + 1], block[2 * t + 1 : 2 * t + 2]], axis=1)


def lane_pick(line, place, shape):
    table = jnp.broadcast_to(line, shape)
    return jnp.take_along_axis(table, place, axis=1, mode="promise_in_bounds")


def force_kernel(blocks, layers, first, last, *refs):
    refs = list(refs)
    outer = layers == (0, 3)
    tab_ref, key_ref = refs[:2]
    wr_ref, wtf_ref, wtop_ref, webf_ref, web_ref, wo_ref = refs[2:8]
    refs = refs[8:]
    if outer:
        below_ref, above_ref = refs.pop(0), refs.pop(0)
    if not first:
        before_ref, site_before_ref = refs[:2]
        refs = refs[2:]
    if last:
        list_ref = refs.pop(0)
    spread_ref, site_ref = refs[:2]
    refs = refs[2:]
    if outer:
        extra_ref = refs.pop(0)
    geo, res, acc, own_sum, table_ref = refs[:5]
    cells = [(block, layer) for block in blocks for layer in layers]
    count = len(cells)
    works, slopes = refs[5 : 5 + count], refs[5 + count :]
    lane48 = lax.broadcasted_iota(jnp.int32, (48, 128), 1)
    if outer:
        wide = jnp.zeros((48, 96), F32)
        below = jnp.concatenate([below_ref[...], wide], axis=1)
        above = pltpu.roll(jnp.concatenate([above_ref[...], wide], axis=1), 96, 1)
        table_ref[0] = jnp.where(lane48 < 32, below, pltpu.roll(tab_ref[...], 32, 1))
        table_ref[1] = jnp.where(lane48 < 96, pltpu.roll(tab_ref[...], 96, 1), above)
    else:
        table_ref[0] = tab_ref[...]
    bases = {0: 0, 1: 32, 2: 32, 3: 64}
    side = {0: 0, 1: 0, 2: 0, 3: 1}
    shape = (ROWS, 128)
    lane = lax.broadcasted_iota(jnp.int32, shape, 1)
    for k, (block, layer) in enumerate(cells):
        cx, cy = block // 2, block % 2
        base = bases[layer]
        own_place = 32 * (layer + 1) - base + lane % 32
        key = key_ref[block, layer]
        col = key >> 8
        place = (key & 255) - base
        own = []
        other = []
        for a in range(3):
            found = None
            for ox in range(3):
                for oy in range(3):
                    c = (cx + ox) * 4 + cy + oy
                    line = table_ref[side[layer], a * 16 + c : a * 16 + c + 1, :]
                    picked = lane_pick(line, place, shape)
                    found = picked if found is None else jnp.where(col == c, picked, found)
                    if ox == 1 and oy == 1:
                        own.append(lane_pick(line, own_place, shape))
            other.append(found)
        usable = jnp.logical_and(own[0] < 0.5 * UNOCCUPIED, other[0] < 0.5 * UNOCCUPIED)
        shift = (
            (col >> 2) - (cx + 1),
            (col & 3) - (cy + 1),
            (place + base) // 32 - (layer + 1),
        )
        far = (FAR, 0.0, 0.0)
        displace = [
            jnp.where(usable, other[a] - own[a] + shift[a].astype(F32), far[a]) for a in range(3)
        ]
        square = displace[0] ** 2 + displace[1] ** 2 + displace[2] ** 2
        radius = jnp.sqrt(square + 0.25)
        inverse = 1.0 / radius
        root = jnp.maximum(1.0 - 0.25 * square, 0.0)
        kept = [radius, root] + [displace[a] * inverse for a in range(3)] + displace
        kept.append(-4.0 * inverse * (root * root))
        for slot, value in enumerate(kept):
            geo[slot, k] = value

    same = lax.broadcasted_iota(jnp.int32, (32, 256), 1) % 32 == lax.broadcasted_iota(
        jnp.int32, (32, 256), 0
    )
    centre = CENTRE_FIRST + CENTRE_STEP * lax.broadcasted_iota(jnp.int32, (BASIS, 256), 0).astype(
        F32
    )

    def pair_of_cells(ks):
        lefts, mixeds, backs = {}, {}, {}
        for k in ks:
            work, slope = works[k], slopes[k]
            radius8 = geo[0, k]
            root8 = geo[1, k]
            scale8 = geo[8, k]
            dir8 = [geo[2 + a, k] for a in range(3)]
            for t in range(TILES):
                lanes = slice(256 * t, 256 * t + 256)
                away = pair_row(radius8, t) - centre
                radial = jnp.exp(-4.0 * away * away)
                steep = radial * (away * pair_row(scale8, t))
                high = radial.astype(BF16).astype(F32)
                steep_high = steep.astype(BF16).astype(F32)
                zero = jnp.zeros_like(high)
                stacked = jnp.concatenate(
                    [high, radial - high, high, zero, steep_high, steep - steep_high, steep_high, zero],
                    axis=0,
                ).astype(BF16)
                both = dot(wr_ref[...], stacked)
                zh = both[0:128]
                th = jnp.tanh(zh)
                up = 1.0 + th
                root = pair_row(root8, t)
                work[0:128, lanes] = (zh * up * (root * root)).astype(BF16)
                slope[:, lanes] = up * (
                    (1.0 + zh * (1.0 - th)) * both[128:256] - zh * (0.5 * root)
                )
                for a in range(3):
                    work[128 + 32 * a : 160 + 32 * a, lanes] = jnp.where(
                        same, pair_row(dir8[a], t), 0.0
                    ).astype(BF16)
                work[224:256, lanes] = jnp.zeros((32, 256), BF16)
        yield
        gathered = [dot_nt(works[k][0:128, :], works[k][128:256, :]).astype(BF16) for k in ks]
        mixed = dot(webf_ref[...], jnp.concatenate(gathered, axis=1))
        for i, k in enumerate(ks):
            part = mixed[:, 128 * i : 128 * i + 128]
            mixeds[k] = (2.0 * part.T).astype(BF16)
            lefts[k] = jnp.concatenate([wtf_ref[...], part.astype(BF16)], axis=1)
        yield
        for k in ks:
            work, left = works[k], lefts[k]
            root8 = geo[1, k]
            for t in range(TILES):
                lanes = slice(256 * t, 256 * t + 256)
                ph = dot(left, work[0:256, lanes])
                th = jnp.tanh(ph)
                up = 1.0 + th
                root = pair_row(root8, t)
                readout = wo_ref[...]
                energy = jnp.sum(readout * (ph * up), axis=0, keepdims=True)
                res[4, k, 2 * t : 2 * t + 1] = energy[:, 0:128]
                res[4, k, 2 * t + 1 : 2 * t + 2] = energy[:, 128:256]
                work[256:384, lanes] = (
                    (readout * (0.5 * root * root)) * (up * (1.0 + ph * (1.0 - th)))
                ).astype(BF16)
        yield
        gathered = [dot_nt(works[k][256:384, :], works[k][128:256, :]).astype(BF16) for k in ks]
        back = dot(web_ref[...], jnp.concatenate(gathered, axis=1))
        for i, k in enumerate(ks):
            part = back[:, 128 * i : 128 * i + 128]
            backs[k] = part.T.astype(BF16)
            lefts[k] = jnp.concatenate(
                [
                    jnp.concatenate([part.astype(BF16), wtop_ref[...]], axis=1),
                    jnp.concatenate([jnp.zeros((96, 128), BF16), mixeds[k][0:96]], axis=1),
                ],
                axis=0,
            )
        yield
        for k in ks:
            work, slope, left, back_t = works[k], slopes[k], lefts[k], backs[k]
            for t in range(TILES):
                lanes = slice(256 * t, 256 * t + 256)
                latent = work[0:128, lanes]
                slant = dot(left, work[128:384, lanes])
                turned = slant[128:224] + dot(back_t[0:96], latent)
                outcome = [
                    jnp.sum(jnp.where(same, turned[32 * a : 32 * a + 32], 0.0), axis=0, keepdims=True)
                    for a in range(3)
                ]
                outcome.append(jnp.sum(slant[0:128] * slope[:, lanes], axis=0, keepdims=True))
                for value, slot in zip(outcome, (0, 1, 2, 3)):
                    res[slot, k, 2 * t : 2 * t + 1] = value[:, 0:128]
                    res[slot, k, 2 * t + 1 : 2 * t + 2] = value[:, 128:256]

    runs = [pair_of_cells((k, k + 1)) for k in range(0, count, 2)]
    done = object()
    for tick in range(6 + len(runs)):
        for number in reversed(range(len(runs))):
            if tick >= number and runs[number] is not None:
                if next(runs[number], done) is done:
                    runs[number] = None

    radius, root = geo[0], geo[1]
    direction = [geo[2 + a] for a in range(3)]
    pull = [res[a] for a in range(3)]
    readout = res[4]
    inverse = 1.0 / radius
    along = pull[0] * direction[0] + pull[1] * direction[1] + pull[2] * direction[2]
    to_square = res[3] - 0.5 * (root * readout + inverse * inverse * along)
    for a in range(3):
        geo[2 + a] = pull[a] * inverse + geo[5 + a] * (2.0 * to_square)
    res[4] = root * root * readout

    acc[...] = jnp.zeros_like(acc)
    iota96 = lax.broadcasted_iota(jnp.int32, (96, 128), 0)
    iota16 = lax.broadcasted_iota(jnp.int32, (16, 128), 0)
    lane1 = lax.broadcasted_iota(jnp.int32, (1, 128), 1)
    own_sum[...] = jnp.zeros_like(own_sum)

    def spread_rows(col_row, terms):
        highs, lows = [], []
        for term in terms:
            chosen = jnp.where(col_row == iota16, term, 0.0)
            high = chosen.astype(BF16)
            highs.append(high)
            lows.append((chosen - high.astype(F32)).astype(BF16))
        return jnp.concatenate(highs + lows, axis=0)

    for k, (block, layer) in enumerate(cells):
        key = key_ref[block, layer]
        col = key >> 8
        place = (key & 255) - 32 * layer
        term = [geo[2 + a, k] for a in range(3)]
        hots, lefts = [], []
        for r in range(USED):
            hots.append(jnp.where(iota96 == place[r : r + 1], 1.0, 0.0).astype(BF16))
            lefts.append(spread_rows(col[r : r + 1], [-term[a][r : r + 1] for a in range(3)]))
        added = dot_nt(jnp.concatenate(hots, axis=1), jnp.concatenate(lefts, axis=1))
        at = 32 * layer - bases[layer]
        acc[side[layer], at : at + 96, 0:96] += added
        term.append(res[4, k])
        for slot in range(4):
            line = jnp.sum(term[slot][0:USED], axis=0, keepdims=True)
            line = line + pltpu.roll(line, 32, 1)
            line = line + pltpu.roll(line, 64, 1)
            own_sum[slot, block : block + 1, :] += jnp.where(lane1 // 32 == layer, line, 0.0)

    flipped = acc[0].T
    total = flipped[0:48] + flipped[48:96]
    if outer:
        flipped = acc[1].T
        upper = flipped[0:48] + flipped[48:96]
        extra_ref[...] = jnp.where(lane48 < 96, total, upper)
        total = jnp.where(lane48 < 96, pltpu.roll(total, 96, 1), 0.0) + jnp.where(
            lane48 >= 32, pltpu.roll(upper, 32, 1), 0.0
        )
    site = own_sum[3]
    if not first:
        total = total + before_ref[...]
        site = site + site_before_ref[...]
    spread_ref[...] = total
    for a in range(3):
        for block in blocks:
            line = a * 16 + (block // 2 + 1) * 4 + block % 2 + 1
            spread_ref[line : line + 1, :] += own_sum[a, block : block + 1, :]
    if not last:
        site_ref[...] = site
    else:
        listed = list_ref[...]
        sent = jnp.zeros((16, 128), F32)
        for block in range(4):
            table = jnp.broadcast_to(site[block : block + 1], (16, 128))
            picked = jnp.take_along_axis(table, listed & 127, axis=1, mode="promise_in_bounds")
            sent = jnp.where(listed >> 7 == block, picked, sent)
        site_ref[...] = sent


def force_call(tab, key, weights, blocks, layers, halo=(), before=None, listed=None):
    first, last = before is None, listed is not None
    count = len(blocks) * len(layers)
    args = [tab, key, *weights, *halo]
    if not first:
        args += before
    if last:
        args.append(listed)
    outs = [48, 16 if last else 8] + [48] * len(halo[:1])
    return pl.pallas_call(
        functools.partial(force_kernel, blocks, layers, first, last),
        out_shape=tuple(jax.ShapeDtypeStruct((rows, 128), F32) for rows in outs),
        scratch_shapes=[
            pltpu.VMEM((9, count, ROWS, 128), F32),
            pltpu.VMEM((5, count, ROWS, 128), F32),
            pltpu.VMEM((2, 128, 128), F32),
            pltpu.VMEM((4, 8, 128), F32),
            pltpu.VMEM((2, 48, 128), F32),
        ]
        + [pltpu.VMEM((384, 768), BF16)] * count
        + [pltpu.VMEM((128, 768), F32)] * count,
        compiler_params=pltpu.CompilerParams(vmem_limit_bytes=40 * 1024 * 1024),
        cost_estimate=pl.CostEstimate(
            flops=count * 800_000_000, bytes_accessed=300_000, transcendentals=0
        ),
        name="force",
    )(*args)


def lanes_below(count_ref, cx, cy):
    lane = lax.broadcasted_iota(jnp.int32, (1, 128), 1)
    limit = jnp.zeros((1, 128), jnp.int32)
    for cz in range(4):
        limit = jnp.where(lane // 32 == cz, count_ref[cx, cy, cz], limit)
    return lane % 32 < limit


def begin_kernel(
    positions_ref, velocities_ref, forces_ref, count_ref, low_ref, high_ref, coords_ref
):
    speed = velocities_ref[...] + 0.5 * TIME_STEP * forces_ref[...]
    coords = positions_ref[...] + TIME_STEP * speed
    coords_ref[...] = coords + TIME_STEP * speed
    for cx, first_ref in enumerate((low_ref, high_ref)):
        first_ref[3:6, 0] = speed[:, cx]
        for cy in range(2):
            occupied = lanes_below(count_ref, cx, cy)
            for a in range(3):
                first_ref[a, 0, cy : cy + 1, :] = jnp.where(
                    occupied, coords[a, cx, cy : cy + 1, :], UNOCCUPIED
                )


def finish_kernel(
    source_ref, x_ref, below_ref, above_ref, pace_ref, place_ref, drift_ref, count_ref, *outs
):
    coords_ref, speed_ref, force_ref, rows_ref, arrived_ref, semaphore = outs
    copy = pltpu.make_async_copy(source_ref, arrived_ref, semaphore)
    copy.start()
    for cx in range(2):
        for cy in range(2):
            occupied = lanes_below(count_ref, cx, cy)
            for a in range(3):
                beside = below_ref if cy == 0 else above_ref
                force = x_ref[a, cx, cy + 1 : cy + 2, :] + beside[a, cx]
                force_ref[a, cx, cy : cy + 1, :] = force
                speed = pace_ref[a, cx + 1, cy + 1 : cy + 2, :]
                speed_ref[a, cx, cy : cy + 1, :] = speed + 0.5 * TIME_STEP * force
                coords_ref[a, cx, cy : cy + 1, :] = jnp.where(
                    occupied,
                    place_ref[a, cx + 1, cy + 1 : cy + 2, :],
                    drift_ref[a, cx, cy : cy + 1, :],
                )
    copy.wait()
    lane = lax.broadcasted_iota(jnp.int32, (1, 128), 1)
    for row in range(4):
        line = arrived_ref[4 * row : 4 * row + 1, :]
        for part in range(1, 4):
            moved = pltpu.roll(arrived_ref[4 * row + part : 4 * row + part + 1, :], 32 * part, 1)
            line = jnp.where(lane // 32 == part, moved, line)
        rows_ref[row : row + 1, :] = line


def prepare_kernel(
    near_ref, list_ref, radial_ref, env_ref, latent_ref, out_ref,
    key_ref, listed_ref, wr_ref, wtf_ref, wtop_ref, webf_ref, web_ref, wo_ref,
):
    lane = lax.broadcasted_iota(jnp.int32, (USED, 128), 1)
    for block in range(4):
        cx, cy = block // 2, block % 2
        codes = [near_ref[USED * part : USED * part + USED, cx, cy, :] for part in range(4)]
        for layer in range(4):
            code = codes[0] if layer == 0 else pltpu.roll(codes[0], 128 - 32 * layer, 1)
            for part in range(1, 4):
                turn = 32 * (part - layer) % 128
                moved = pltpu.roll(codes[part], turn, 1) if turn else codes[part]
                code = jnp.where(lane // 32 == part, moved, code)
            offset = code >> 5
            third = (offset * 43) >> 7
            ninth = (third * 43) >> 7
            col = (cx + ninth) * 4 + cy + third - 3 * ninth
            place = (layer + offset - 3 * third) * 32 + (code & 31)
            key_ref[block, layer] = jnp.concatenate(
                [col * 256 + place, jnp.zeros((ROWS - USED, 128), jnp.int32)], axis=0
            )
    for row in range(16):
        line = list_ref[0, :, 128 * (row // 4) : 128 * (row // 4) + 128]
        turn = 32 * (-row % 4)
        listed_ref[row : row + 1, :] = pltpu.roll(line, turn, 1) if turn else line
    radial = 0.5 * radial_ref[...]
    high = radial.astype(BF16).astype(F32)
    zero = jnp.zeros_like(high)
    parts = [high, high, radial - high, zero]
    wr_ref[0:128, :] = jnp.concatenate(parts + [zero] * 12, axis=0).T[:, 0:64].astype(BF16)
    wr_ref[128:256, :] = (
        jnp.concatenate([zero] * 4 + parts + [zero] * 8, axis=0).T[:, 0:64].astype(BF16)
    )
    top = latent_ref[0:128, :]
    wtop_ref[...] = top
    wtf_ref[...] = (0.5 * top.astype(F32)).T.astype(BF16)
    both = dot(env_ref[...], latent_ref[128:256, :])
    web_ref[...] = both.astype(BF16)
    webf_ref[...] = (0.5 * both).T.astype(BF16)
    readout = jnp.broadcast_to(out_ref[...].astype(F32), (128, 128)).T
    wo_ref[:, 0:128] = readout
    wo_ref[:, 128:256] = readout


def prepare(neighbours, send_list, w_radial, w_env, w_latent, w_out):
    square = jax.ShapeDtypeStruct((128, 128), BF16)
    key, listed, *weights = pl.pallas_call(
        prepare_kernel,
        out_shape=(
            jax.ShapeDtypeStruct((4, 4, ROWS, 128), jnp.int32),
            jax.ShapeDtypeStruct((16, 128), jnp.int32),
            jax.ShapeDtypeStruct((256, 64), BF16),
            square,
            square,
            square,
            square,
            jax.ShapeDtypeStruct((128, 256), F32),
        ),
        name="prepare",
    )(neighbours, send_list, w_radial, w_env, w_latent, w_out.reshape(1, 128))
    return key, listed, weights


def shifted(array, axis, step):
    peers = lax.axis_size(axis)
    return lax.ppermute(array, axis, [(i, (i + step) % peers) for i in range(peers)])


def both_ways(array, axis, dim, low, high):
    from_below = shifted(lax.slice_in_dim(array, *high, axis=dim), axis, 1)
    from_above = shifted(lax.slice_in_dim(array, *low, axis=dim), axis, -1)
    return from_below, from_above


def with_halo(array, axis, dim):
    below, above = both_ways(array, axis, dim, (0, 1), (1, 2))
    return jnp.concatenate([below, array, above], axis=dim)


def share(padded, axis, dim):
    below, above = both_ways(padded, axis, dim, (0, 2), (2, 4))
    return padded + jnp.concatenate([below, above], axis=dim)


def on_device(
    positions,
    velocities,
    forces_in,
    counts,
    neighbours,
    send_list,
    w_radial,
    w_env,
    w_latent,
    w_out,
):
    key, listed, weights = prepare(neighbours, send_list, w_radial, w_env, w_latent, w_out)
    half = TIME_STEP
    own = jax.ShapeDtypeStruct((3, 2, 2, 128), F32)
    vmem, smem = (pl.BlockSpec(memory_space=space) for space in (pltpu.VMEM, pltpu.SMEM))
    face = jax.ShapeDtypeStruct((6, 1, 2, 128), F32)
    low, high, drift = pl.pallas_call(
        begin_kernel,
        out_shape=(face, face, own),
        in_specs=[vmem] * 3 + [smem],
        name="begin",
    )(positions, velocities, forces_in, counts)
    first = jnp.concatenate([shifted(high, "gx", 1), low, high, shifted(low, "gx", -1)], axis=1)
    first = with_halo(first, "gy", 2)

    def one_step(repeat, carry):
        wide_coords, wide_speed, force = carry[0:3]

        def from_force(part):
            part = share(share(part, "gx", 1), "gy", 2)
            return jnp.concatenate([half * half * part, half * part], axis=0)

        change = lax.cond(repeat == 0, lambda part: first, from_force, force)
        wide_coords = wide_coords + half * wide_speed + change[0:3]
        wide_speed = wide_speed + change[3:6]
        flat = wide_coords.reshape(48, 128)
        halo = shifted(flat[:, 96:128], "gz", 1), shifted(flat[:, 0:32], "gz", -1)
        state = force_call(flat, key, weights, (0, 1), (1, 2))
        *state, rim = force_call(flat, key, weights, (0, 1, 2, 3), (0, 3), halo, state)
        from_below = shifted(rim[:, 96:128], "gz", 1)
        from_above = shifted(rim[:, 0:32], "gz", -1)
        spread, sent = force_call(
            flat, key, weights, (2, 3), (1, 2), before=state, listed=listed
        )
        edges = jnp.concatenate([from_below, jnp.zeros((48, 64), F32), from_above], axis=1)
        force = (spread + edges).reshape(3, 4, 4, 128)
        return (wide_coords, wide_speed, force, force[:, 0:1], force[:, 3:4], sent)

    zero = jnp.zeros((3, 4, 4, 128), F32)
    carry = (zero, zero, zero, zero[:, 0:1], zero[:, 0:1], jnp.zeros((16, 128), F32))
    wide_coords, wide_speed, force, low, high, sent = lax.fori_loop(0, STEPS, one_step, carry)
    work_energy = lax.all_to_all(sent, "gz", split_axis=0, concat_axis=0, tiled=True)
    force = force[:, 1:3] + jnp.concatenate(
        [shifted(high, "gx", 1), shifted(low, "gx", -1)], axis=1
    )
    below, above = both_ways(force, "gy", 2, (0, 1), (3, 4))
    *moved, rows = pl.pallas_call(
        finish_kernel,
        out_shape=(own, own, own, jax.ShapeDtypeStruct((4, 128), F32)),
        in_specs=[pl.BlockSpec(memory_space=pltpu.HBM)] + [vmem] * 6 + [smem],
        scratch_shapes=[pltpu.VMEM((16, 128), F32), pltpu.SemaphoreType.DMA(())],
        name="finish",
    )(work_energy, force, below, above, wide_speed, wide_coords, drift, counts)
    return (*moved, rows.reshape(1, 1, 512))


def solution(mesh):
    split = P(None, "gx", "gy", "gz")
    cells = P("gx", "gy", "gz")
    return jax.shard_map(
        on_device,
        mesh=mesh,
        in_specs=(split, split, split, cells, split, cells, P(), P(), P(), P()),
        out_specs=(split, split, split, cells),
        check_vma=False,
    )
```
